512 devices in a mesh: row: 32 (over x, z), col: 16 (over y, core).
Axes of the slice: x: 4, y: 8, z: 8, core: 2. Of those that a mesh axis runs over, the one named last changes fastest.
Arguments:
- positions: float32 [3, 32768], P(None, ('row', 'col')), may hold values from -0.3 to 31.3, as said below
- species: int32 [32768], P(('row', 'col')), may hold values from 0 to 3
- hardness: float32 [4], replicated, may hold values from 1 to 3
- gauss_width: float32 [4], replicated, may hold values from 0.5 to 1.5
- charges: float32 [32768], P(('row', 'col')), may hold values from -3 to 3
- cotangent: float32 [8, 32768], P(None, ('row', 'col')), may hold values from -21 to 21
- warm_start: float32 [8, 32768], P(None, ('row', 'col')), may hold values from -1.8 to 1.8
Outputs:
- adjoint: float32 [8, 32768], P(None, ('row', 'col'))
- coord_grad: float32 [8, 3, 32768], P(None, None, ('row', 'col'))
The draws below stay inside these ranges and needn't reach their ends.
Inputs may be any that keep to these rules, and one draw needn't show every extreme that they name: `positions`: atom n lies within 0.3 in each coordinate of the lattice point (n mod 32, (n div 32) mod 32, n div (1024)); hence any two atoms are 0.4 or more apart.
All inputs are finite; a program needn't handle non-finite values.
Results may differ from the reference program's by a relative error of at most 0.0003.
Values sent between devices are 32-bit elements; how exact they have to be, the bound alone decides.
A program may use at most 64 MiB of HBM per device.

```python
import math
import jax
import jax.numpy as jnp
from jax import lax

RHS = 8
SPECIES = 4
PLANE = 32
ITERS = 2
ATOMS = 32768


def draw_positions(key, part):
    key = jax.random.fold_in(key, 11)
    atom_index = jnp.arange(ATOMS, dtype=jnp.int32)
    lattice = jnp.stack([atom_index % PLANE, atom_index // PLANE % PLANE, atom_index // (PLANE * PLANE)]).astype(jnp.float32)
    jitter = jnp.clip(0.12 * jax.random.normal(key, (3, ATOMS), jnp.float32), -0.3, 0.3)
    return lattice + jitter


def draw_cotangent(key, part):
    key = jax.random.fold_in(key, 23)
    ramp = jnp.exp(jnp.log(3.0) * jnp.arange(ATOMS, dtype=jnp.float32) / ATOMS)
    values = jnp.clip(jax.random.normal(key, (RHS, ATOMS), jnp.float32), -4.0, 4.0)
    return values * ramp[None, :]


def plant(values, key, low, top_value):
    index_at = [jax.random.randint(jax.random.fold_in(key, axis), (), 0, length) for axis, length in enumerate(values.shape)]
    main_axis = values.shape.index(max(values.shape))
    next_to = index_at[:main_axis] + [(index_at[main_axis] + 1) % values.shape[main_axis]] + index_at[main_axis + 1:]
    return values.at[tuple(index_at)].set(low).at[tuple(next_to)].set(top_value)


def block_levels(own_key, dims, cuts, smallest, high):
    gain = 1.0
    for dim, shards_of in cuts:
        draws = jax.random.uniform(jax.random.fold_in(jax.random.fold_in(own_key, 6), dim), (shards_of,), jnp.float32, smallest / len(cuts), high / len(cuts))
        gain = gain * jnp.repeat(jnp.exp(draws), dims[dim] // shards_of).reshape((-1,) + (1,) * (len(dims) - 1 - dim))
    return gain


def scatter_about(stream_key, extent, scale, limit, pieces=(), held_as=jnp.bfloat16):
    values = jax.random.normal(stream_key, extent, jnp.float32) * scale
    if len(pieces) > 0:
        values = block_levels(stream_key, extent, pieces, -0.22, 0.18) * values
    return jnp.clip(values, min=-limit, max=limit).astype(held_as)


def setup_inputs(seed: int = 0) -> dict:
    streams_of = jax.random.split(jax.random.key(seed), 8)
    return {
        "positions": draw_positions(jax.random.fold_in(streams_of[7], 71), 0),
        "species": plant(jax.random.randint(streams_of[1], (ATOMS,), 0, SPECIES), jax.random.fold_in(streams_of[1], 1), 0, SPECIES - 1).astype(jnp.int32),
        "hardness": jnp.clip(jax.random.uniform(streams_of[2], (SPECIES,), jnp.float32, 1.0, 3.0), 1.0, 3.0),
        "gauss_width": jnp.clip(jax.random.uniform(streams_of[3], (SPECIES,), jnp.float32, 0.5, 1.5), 0.5, 1.5),
        "charges": scatter_about(streams_of[4], (ATOMS,), 0.5, 3.0, ((0, 512),), jnp.float32),
        "cotangent": draw_cotangent(jax.random.fold_in(streams_of[7], 71), 0),
        "warm_start": scatter_about(streams_of[6], (RHS, ATOMS), 0.3, 1.8, ((1, 512),), jnp.float32),
    }


ROOT_PI = math.sqrt(math.pi)
EXACT = lax.Precision.HIGHEST

def species_values(species, hardness, gauss_width):
    onehot_table = (species[:, None] == jnp.arange(hardness.shape[0], dtype=jnp.int32)[None, :]).astype(jnp.float32)
    return (lax.optimization_barrier(jnp.sum(onehot_table * hardness[None, :], axis=1)), lax.optimization_barrier(jnp.sum(onehot_table * gauss_width[None, :], axis=1)))

def pair_geometry(row_geo, col_geo, same_atom):
    square = jnp.zeros(same_atom.shape, jnp.float32)
    for axis_no in range(3):
        offset = row_geo[axis_no][:, None] - col_geo[axis_no][None, :]
        square = square + offset * offset
    square = jnp.where(same_atom, jnp.float32(1.0), square)
    spread = row_geo[3][:, None] * row_geo[3][:, None] + col_geo[3][None, :] * col_geo[3][None, :]
    return (square, lax.rsqrt(2.0 * spread))

def coulomb(row_geo, col_geo, same_atom):
    square, inverse = pair_geometry(row_geo, col_geo, same_atom)
    distance = jnp.sqrt(square)
    return jnp.where(same_atom, jnp.float32(0.0), lax.erf(inverse * distance) / distance)

def slope(row_geo, col_geo, same_atom):
    square, inverse = pair_geometry(row_geo, col_geo, same_atom)
    distance = jnp.sqrt(square)
    result = 2.0 / ROOT_PI * inverse * jnp.exp(-inverse * inverse * square) / square - lax.erf(inverse * distance) / (square * distance)
    return jnp.where(same_atom, jnp.float32(0.0), result)

def apply_matrix(vectors, geometry, diagonal):
    block_size = math.gcd(ATOMS, 512)
    atom_index = jnp.arange(ATOMS, dtype=jnp.int32)

    def one_block(block_no):
        first_row = block_no * block_size
        row_geo = lax.dynamic_slice_in_dim(geometry, first_row, block_size, 1)
        row_index = first_row + jnp.arange(block_size, dtype=jnp.int32)
        kernel = coulomb(row_geo, geometry, row_index[:, None] == atom_index[None, :])
        return jnp.einsum('ij,rj->ri', kernel, vectors, precision=EXACT)
    blocks_out = lax.map(one_block, jnp.arange(ATOMS // block_size, dtype=jnp.int32))
    return jnp.transpose(blocks_out, (1, 0, 2)).reshape(vectors.shape) + diagonal[None, :] * vectors

def coord_gradient(adjoint, geometry):
    block_size = math.gcd(ATOMS, 512)
    atom_index = jnp.arange(ATOMS, dtype=jnp.int32)
    points = geometry[:3]
    charge_row = geometry[4]
    weights = jnp.concatenate([charge_row[None, :], charge_row[None, :] * points, adjoint, (adjoint[:, None, :] * points[None, :, :]).reshape(3 * RHS, ATOMS)], axis=0)

    def one_block(block_no):
        first_row = block_no * block_size
        row_geo = lax.dynamic_slice_in_dim(geometry, first_row, block_size, 1)
        row_adj = lax.dynamic_slice_in_dim(adjoint, first_row, block_size, 1)
        row_index = first_row + jnp.arange(block_size, dtype=jnp.int32)
        slopes = slope(row_geo, geometry, row_index[:, None] == atom_index[None, :])
        sums = jnp.einsum('ij,wj->wi', slopes, weights, precision=EXACT)
        row_points = row_geo[:3]
        first_sum = sums[0]
        moment = sums[1:4]
        adj_sum = sums[4:4 + RHS]
        adj_moment = sums[4 + RHS:].reshape(RHS, 3, block_size)
        return -(row_adj[:, None, :] * (row_points[None] * first_sum[None, None, :] - moment[None]) + row_geo[4][None, None, :] * (row_points[None] * adj_sum[:, None, :] - adj_moment))
    blocks_out = lax.map(one_block, jnp.arange(ATOMS // block_size, dtype=jnp.int32))
    return jnp.transpose(blocks_out, (1, 2, 0, 3)).reshape(RHS, 3, ATOMS)

def reference(positions, species, hardness, gauss_width, charges, cotangent, warm_start):
    hard_atom, wide_atom = species_values(species, hardness, gauss_width)
    diagonal = hard_atom + 1.0 / (wide_atom * ROOT_PI)
    geometry = jnp.concatenate([positions, wide_atom[None, :], charges[None, :]], axis=0)
    adjoint = warm_start
    residual = cotangent - apply_matrix(warm_start, geometry, diagonal)
    direction = residual
    norm_now = lax.optimization_barrier(jnp.sum(residual * residual, axis=1))
    for turn_no in range(ITERS):
        applied = apply_matrix(direction, geometry, diagonal)
        step_size = norm_now / lax.optimization_barrier(jnp.sum(direction * applied, axis=1))
        adjoint = adjoint + step_size[:, None] * direction
        if turn_no + 1 < ITERS:
            residual = residual - step_size[:, None] * applied
            norm_next = lax.optimization_barrier(jnp.sum(residual * residual, axis=1))
            direction = residual + (norm_next / norm_now)[:, None] * direction
            norm_now = norm_next
    return (adjoint, coord_gradient(adjoint, geometry))
```

```python
import functools
import math

import jax
import jax.numpy as jnp
from jax import lax
from jax.experimental import pallas as pl
from jax.experimental.pallas import tpu as pltpu
from jax.sharding import PartitionSpec as P

MESH = pl.DeviceIdType.MESH
F32 = jnp.float32
BF16 = jnp.bfloat16
ROOT_PI = math.sqrt(math.pi)
OWN = 64
WIDE = 128
CENTRE = 16.0


def split(x):
    hi = x.astype(BF16).astype(F32)
    return jnp.concatenate([hi, x - hi], axis=0).astype(BF16)


def fold(x):
    half = x.shape[0] // 2
    return x[:half] + x[half:]


def pair_up(first, second):
    low = lax.broadcasted_iota(jnp.int32, first.shape, first.ndim - 1) < OWN
    axis = first.ndim - 1
    return (
        jnp.where(low, first, pltpu.roll(second, OWN, axis)),
        jnp.where(low, pltpu.roll(first, OWN, axis), second),
    )


def kernel(
    rows, cols,
    hard_ref, width_ref, pos_ref, species_ref, charge_ref, cot_ref, warm_ref,
    adj_out, grad_out,
    own_geo, own_vec, own_tmp,
    col_g, row_g, col_p, row_p, col_v, row_v, col_w, row_w, col_q, row_q, col_t, row_t, col_s, row_s,
    scal, geo_i, geo_j, vec_i, vec_j, out_i, out_j, grad_i, grad_j,
    bcast, k_hi, k_lo, h_hi, h_lo,
    send_sem, recv_sem,
):
    half = rows // 2
    chunks = half + 1
    pairs = (chunks + 1) // 2
    tiles = cols // 2
    row = lax.axis_index("row")
    col = lax.axis_index("col")

    def at_col(shift):
        return {"col": lax.rem(col + shift + cols, cols)}

    def at_row(shift):
        return {"row": lax.rem(row + shift + rows, rows)}

    barrier = pltpu.get_barrier_semaphore()

    @pl.loop(1, cols)
    def _(m):
        pl.semaphore_signal(barrier, inc=1, device_id=at_col(m), device_id_type=MESH)

    @pl.loop(1, rows)
    def _(k):
        pl.semaphore_signal(barrier, inc=1, device_id=at_row(k), device_id_type=MESH)

    lane = lax.broadcasted_iota(jnp.int32, (8, WIDE), 1)
    sub = lax.broadcasted_iota(jnp.int32, (8, WIDE), 0)
    low = lane < OWN
    species = species_ref[...]
    hard = jnp.zeros((1, OWN), F32)
    wide = jnp.zeros((1, OWN), F32)
    for s in range(4):
        hard = hard + jnp.where(species == s, hard_ref[s], 0.0)
        wide = wide + jnp.where(species == s, width_ref[s], 0.0)
    own_geo[...] = jnp.zeros((8, WIDE), F32)
    own_geo[0:3, 0:OWN] = pos_ref[...]
    own_geo[3:4, 0:OWN] = 2.0 * wide * wide
    own_geo[4:5, 0:OWN] = charge_ref[...]
    own_geo[5:6, 0:OWN] = hard + 1.0 / (wide * ROOT_PI)
    own_vec[...] = jnp.zeros((3, 8, WIDE), F32)
    own_vec[0, :, 0:OWN] = warm_ref[...]
    own_tmp[...] = jnp.zeros((8, WIDE), F32)
    own_tmp[:, 0:OWN] = cot_ref[...]
    own = own_geo[...] + pltpu.roll(own_vec[0], OWN, 1)
    col_g[0] = own
    row_g[0] = own

    pl.semaphore_wait(barrier, cols + rows - 2)

    def copies(phase, src_col, src_row, dst_col, dst_row, sign, row_count):
        @pl.loop(1, cols)
        def _(m):
            pltpu.make_async_remote_copy(
                src_ref=src_col(m), dst_ref=dst_col.at[m],
                send_sem=send_sem.at[2 * phase], recv_sem=recv_sem.at[2 * phase],
                device_id=at_col(sign * m), device_id_type=MESH,
            ).start()

        @pl.loop(1, row_count)
        def _(k):
            pltpu.make_async_remote_copy(
                src_ref=src_row(k), dst_ref=dst_row.at[k],
                send_sem=send_sem.at[2 * phase + 1], recv_sem=recv_sem.at[2 * phase + 1],
                device_id=at_row(sign * k), device_id_type=MESH,
            ).start()

    def whole(buffer, count, sem):
        part = buffer.at[pl.ds(1, count - 1)]
        return pltpu.make_async_copy(part, part, sem)

    def wait_col(phase, dst_col):
        whole(dst_col, cols, recv_sem.at[2 * phase]).wait()

    def wait_row(phase, dst_row, row_count):
        whole(dst_row, row_count, recv_sem.at[2 * phase + 1]).wait()

    def wait_sent(phase, dst_col, dst_row, row_count):
        whole(dst_col, cols, send_sem.at[2 * phase]).wait()
        whole(dst_row, row_count, send_sem.at[2 * phase + 1]).wait()

    def gather(phase, dst_col, dst_row):
        copies(phase, lambda m: dst_col.at[0], lambda k: dst_row.at[0], dst_col, dst_row, -1, chunks)

    def scatter(phase, src_i, src_j, dst_col, dst_row):
        copies(phase, lambda m: src_i.at[m // 2], lambda k: src_j.at[k // 2], dst_col, dst_row, 1, chunks)

    def gathered_sum(src_i, src_j, dst_col, dst_row):
        even = src_i[0] + src_j[0]
        odd = jnp.zeros_like(even)
        for m in range(1, cols):
            if m % 2:
                odd = odd + dst_col[m]
            else:
                even = even + dst_col[m]
        for k in range(1, chunks):
            if k % 2:
                odd = odd + dst_row[k]
            else:
                even = even + dst_row[k]
        return even + pltpu.roll(odd, OWN, even.ndim - 1)

    def chunk_weight(v):
        def of(k):
            return jnp.where((k == 0) | (k == half), 0.5, jnp.where(k > half, 0.0, 1.0)).astype(F32)

        return jnp.where(low, of(2 * v), of(2 * v + 1))

    gather(0, col_g, row_g)
    for k in range(chunks, 2 * pairs):
        row_g[k] = jnp.full((8, WIDE), 100.0, F32)
        row_v[k] = jnp.zeros((8, WIDE), F32)
        row_w[k] = jnp.zeros((8, WIDE), F32)
    wait_col(0, col_g)
    for u in range(tiles):
        geo, vec = pair_up(col_g[2 * u], col_g[2 * u + 1])
        geo_i[u] = geo
        vec_i[0, u] = vec
    wait_row(0, row_g, chunks)

    def spread(slot):
        return split(jnp.concatenate([vec_i[slot, u] for u in range(tiles)], axis=1))

    def products(v, columns, vec, hi, lo):
        over_rows = split(vec * chunk_weight(v))
        wide_out = jnp.dot(over_rows, hi, preferred_element_type=F32)
        wide_out = wide_out + jnp.dot(over_rows, lo, preferred_element_type=F32)
        nt = (((1,), (1,)), ((), ()))
        tall_out = lax.dot_general(columns, hi, nt, preferred_element_type=F32)
        tall_out = tall_out + lax.dot_general(columns, lo, nt, preferred_element_type=F32)
        return fold(wide_out), fold(tall_out) * chunk_weight(v)

    def put_i(slot, total):
        for u in range(tiles):
            out_i[slot, u] = total[:, u * WIDE:(u + 1) * WIDE]

    columns = spread(0)

    def make_block(v, total):
        geo, vec = pair_up(row_g[2 * v], row_g[2 * v + 1])
        geo_j[v] = geo
        vec_j[0, v] = vec
        tall = jnp.transpose(geo)
        for f in range(4):
            bcast[f] = jnp.broadcast_to(tall[:, f:f + 1], (WIDE, WIDE))
        first = pl.multiple_of(v * WIDE, WIDE)
        for u in range(tiles):
            for s in range(2):
                part = pl.ds(s * OWN, OWN)
                dx = bcast[0, part, :] - geo_i[u, 0:1, :]
                dy = bcast[1, part, :] - geo_i[u, 1:2, :]
                dz = bcast[2, part, :] - geo_i[u, 2:3, :]
                square = dx * dx + dy * dy + dz * dz
                inverse = lax.rsqrt(bcast[3, part, :] + geo_i[u, 3:4, :])
                if u == 0 and s == 0:
                    r = lax.broadcasted_iota(jnp.int32, (OWN, WIDE), 0)
                    l = lax.broadcasted_iota(jnp.int32, (OWN, WIDE), 1)
                    same = (r == l) & (v == 0)
                    square = jnp.where(same, 1.0, square)
                recip = lax.rsqrt(square)
                x = inverse * (square * recip)
                kk = lax.erf(x) * recip
                hh = ((2.0 / ROOT_PI) * inverse * jnp.exp(-(x * x)) - kk) * (recip * recip)
                if u == 0 and s == 0:
                    kk = jnp.where(same, 0.0, kk)
                    hh = jnp.where(same, 0.0, hh)
                at = (pl.ds(first + s * OWN, OWN), pl.ds(u * WIDE, WIDE))
                kk_hi = kk.astype(BF16)
                k_hi[at] = kk_hi
                k_lo[at] = (kk - kk_hi.astype(F32)).astype(BF16)
                hh_hi = hh.astype(BF16)
                h_hi[at] = hh_hi
                h_lo[at] = (hh - hh_hi.astype(F32)).astype(BF16)
        block = pl.ds(first, WIDE)
        wide_out, tall_out = products(v, columns, vec, k_hi[block, :], k_lo[block, :])
        out_j[0, v] = tall_out
        return total + wide_out

    put_i(0, lax.fori_loop(0, pairs, make_block, jnp.zeros((8, tiles * WIDE), F32)))

    diagonal = jnp.where(low, own_geo[5:6, :], 0.0)

    def applied(phase, slot, dst_col, dst_row):
        scatter(phase, out_i.at[slot], out_j.at[slot], dst_col, dst_row)
        wait_col(phase, dst_col)
        wait_row(phase, dst_row, chunks)
        total = gathered_sum(out_i.at[slot], out_j.at[slot], dst_col, dst_row)
        return jnp.where(low, total, 0.0) + diagonal * own_vec[slot]

    def spread_own(phase, slot, dst_col, dst_row):
        dst_col[0] = own_vec[slot]
        dst_row[0] = own_vec[slot]
        gather(phase, dst_col, dst_row)
        wait_col(phase, dst_col)
        for u in range(tiles):
            vec_i[slot, u] = pair_up(dst_col[2 * u], dst_col[2 * u + 1])[0]
        wait_row(phase, dst_row, chunks)
        for v in range(pairs):
            vec_j[slot, v] = pair_up(dst_row[2 * v], dst_row[2 * v + 1])[0]

    own_vec[1] = jnp.where(low, own_tmp[...], 0.0) - applied(1, 0, col_p, row_p)
    spread_own(2, 1, col_v, row_v)

    columns_1 = spread(1)

    def block_1(v, total):
        block = pl.ds(pl.multiple_of(v * WIDE, WIDE), WIDE)
        wide_out, tall_out = products(v, columns_1, vec_j[1, v], k_hi[block, :], k_lo[block, :])
        out_j[1, v] = tall_out
        return total + wide_out

    put_i(1, lax.fori_loop(0, pairs, block_1, jnp.zeros((8, tiles * WIDE), F32)))
    own_vec[2] = applied(3, 1, col_q, row_q)
    spread_own(4, 2, col_w, row_w)

    def block_2(v, total):
        block = pl.ds(pl.multiple_of(v * WIDE, WIDE), WIDE)
        over_rows = split(vec_j[2, v] * chunk_weight(v))
        out = jnp.dot(over_rows, k_hi[block, :], preferred_element_type=F32)
        out = out + jnp.dot(over_rows, k_lo[block, :], preferred_element_type=F32)
        return total + fold(out)

    image = lax.fori_loop(0, pairs, block_2, jnp.zeros((8, tiles * WIDE), F32))
    form = jnp.zeros((8, WIDE), F32)
    for u in range(tiles):
        form = form + vec_i[2, u] * image[:, u * WIDE:(u + 1) * WIDE]
    first = own_vec[1]
    second = own_vec[2]
    form = 2.0 * form + diagonal * second * second

    def at_lane(n, values):
        return jnp.where(lane == n, jnp.sum(values, axis=1, keepdims=True), 0.0)

    scal[0] = (
        at_lane(0, first * first) + at_lane(1, first * second) + at_lane(2, second * second) + at_lane(3, form)
    )

    @pl.loop(1, cols)
    def _(m):
        pltpu.make_async_remote_copy(
            src_ref=scal.at[0], dst_ref=col_s.at[m], send_sem=send_sem.at[10], recv_sem=recv_sem.at[10],
            device_id=at_col(m), device_id_type=MESH,
        ).start()

    wait_col(5, col_s)
    total = scal[0]
    for m in range(1, cols):
        total = total + col_s[m]
    scal[1] = total

    @pl.loop(1, rows)
    def _(k):
        pltpu.make_async_remote_copy(
            src_ref=scal.at[1], dst_ref=row_s.at[k], send_sem=send_sem.at[11], recv_sem=recv_sem.at[11],
            device_id=at_row(k), device_id_type=MESH,
        ).start()

    wait_row(5, row_s, rows)
    for k in range(1, rows):
        total = total + row_s[k]
    norm_0, curve_0, square_w, form_w = (total[:, n:n + 1] for n in range(4))
    alpha_0 = norm_0 / curve_0
    norm_1 = norm_0 - 2.0 * alpha_0 * curve_0 + alpha_0 * alpha_0 * square_w
    grow = 1.0 + norm_1 / norm_0
    curve_1 = grow * grow * curve_0 - 2.0 * grow * alpha_0 * square_w + alpha_0 * alpha_0 * form_w
    alpha_1 = norm_1 / curve_1
    with_first = alpha_0 + alpha_1 * grow
    with_second = -alpha_1 * alpha_0
    own_adj = own_vec[0] + with_first * first + with_second * second
    adj_out[...] = own_adj[:, 0:OWN]

    nt = (((1,), (1,)), ((), ()))

    def moment_rows(geo, adj):
        spots = geo - CENTRE
        charge = geo[4:5, :] * jnp.where(sub < 3, spots, jnp.where(sub == 3, 1.0, 0.0))
        return jnp.concatenate([adj] + [adj * spots[c:c + 1, :] for c in range(3)] + [charge], axis=0)

    def differences(geo, sums):
        spots = geo - CENTRE
        out = [spots[c:c + 1, :] * sums[0:8] - sums[8 + 8 * c:16 + 8 * c] for c in range(3)]
        return jnp.concatenate(out + [spots * sums[35:36] - sums[32:40]], axis=0)

    wide_rows = [
        moment_rows(geo_i[u], vec_i[0, u] + with_first * vec_i[1, u] + with_second * vec_i[2, u]) for u in range(tiles)
    ]
    wide_rows = split(jnp.concatenate(wide_rows, axis=1))

    def grad_block(v, total):
        block = pl.ds(pl.multiple_of(v * WIDE, WIDE), WIDE)
        weight = chunk_weight(v)[0:1, :]
        geo = geo_j[v]
        adj = vec_j[0, v] + with_first * vec_j[1, v] + with_second * vec_j[2, v]
        tall_rows = split(moment_rows(geo, adj) * weight)
        out = jnp.dot(tall_rows, h_hi[block, :], preferred_element_type=F32)
        out = out + jnp.dot(tall_rows, h_lo[block, :], preferred_element_type=F32)
        back = lax.dot_general(wide_rows, h_hi[block, :], nt, preferred_element_type=F32)
        back = back + lax.dot_general(wide_rows, h_lo[block, :], nt, preferred_element_type=F32)
        grad_j[v] = differences(geo, fold(back)) * weight
        return total + fold(out)

    sums = lax.fori_loop(0, pairs, grad_block, jnp.zeros((40, tiles * WIDE), F32))
    for u in range(tiles):
        grad_i[u] = differences(geo_i[u], sums[:, u * WIDE:(u + 1) * WIDE])
    scatter(6, grad_i, grad_j, col_t, row_t)
    wait_col(6, col_t)
    wait_row(6, row_t, chunks)
    sums = gathered_sum(grad_i, grad_j, col_t, row_t)
    charges = own_geo[4:5, :]
    for c in range(3):
        grad = -(own_adj * sums[24 + c:25 + c, :] + charges * sums[8 * c:8 * c + 8, :])
        grad_out[c] = grad[:, 0:OWN]

    wait_sent(0, col_g, row_g, chunks)
    wait_sent(1, col_p, row_p, chunks)
    wait_sent(2, col_v, row_v, chunks)
    wait_sent(3, col_q, row_q, chunks)
    wait_sent(4, col_w, row_w, chunks)
    wait_sent(5, col_s, row_s, rows)
    wait_sent(6, col_t, row_t, chunks)


def solution(mesh):
    rows = mesh.shape["row"]
    cols = mesh.shape["col"]
    chunks = rows // 2 + 1
    pairs = (chunks + 1) // 2
    tiles = cols // 2

    def local(positions, species, hardness, gauss_width, charges, cotangent, warm_start):
        def buffer(*shape):
            return pltpu.VMEM(shape, F32)

        vmem = pl.BlockSpec(memory_space=pltpu.VMEM)
        smem = pl.BlockSpec(memory_space=pltpu.SMEM)
        adjoint, grad = pl.pallas_call(
            functools.partial(kernel, rows, cols),
            out_shape=(
                jax.ShapeDtypeStruct((8, OWN), F32),
                jax.ShapeDtypeStruct((3, 8, OWN), F32),
            ),
            in_specs=[smem, smem] + [vmem] * 5,
            out_specs=(vmem, vmem),
            scratch_shapes=[
                buffer(8, WIDE),
                buffer(3, 8, WIDE),
                buffer(8, WIDE),
                buffer(cols, 8, WIDE), buffer(2 * pairs, 8, WIDE),
                buffer(cols, 8, WIDE), buffer(chunks, 8, WIDE),
                buffer(cols, 8, WIDE), buffer(2 * pairs, 8, WIDE),
                buffer(cols, 8, WIDE), buffer(2 * pairs, 8, WIDE),
                buffer(cols, 8, WIDE), buffer(chunks, 8, WIDE),
                buffer(cols, 32, WIDE), buffer(chunks, 32, WIDE),
                buffer(cols, 8, WIDE), buffer(rows, 8, WIDE),
                buffer(2, 8, WIDE),
                buffer(tiles, 8, WIDE), buffer(pairs, 8, WIDE),
                buffer(3, tiles, 8, WIDE), buffer(3, pairs, 8, WIDE),
                buffer(2, tiles, 8, WIDE), buffer(2, pairs, 8, WIDE),
                buffer(tiles, 32, WIDE), buffer(pairs, 32, WIDE),
                buffer(4, WIDE, WIDE),
            ]
            + [pltpu.VMEM((pairs * WIDE, tiles * WIDE), BF16)] * 4
            + [pltpu.SemaphoreType.DMA((14,)), pltpu.SemaphoreType.DMA((14,))],
            compiler_params=pltpu.CompilerParams(
                collective_id=0, has_side_effects=True, vmem_limit_bytes=40 * 1024 * 1024
            ),
        )(
            hardness, gauss_width, positions, species.reshape(1, OWN), charges.reshape(1, OWN), cotangent, warm_start
        )
        return adjoint, jnp.transpose(grad, (1, 0, 2))

    return jax.shard_map(
        local,
        mesh=mesh,
        in_specs=(
            P(None, ("row", "col")),
            P(("row", "col")),
            P(),
            P(),
            P(("row", "col")),
            P(None, ("row", "col")),
            P(None, ("row", "col")),
        ),
        out_specs=(P(None, ("row", "col")), P(None, None, ("row", "col"))),
        check_vma=False,
    )
```

```python
import functools
import math

import jax
import jax.numpy as jnp
from jax import lax
from jax.experimental import pallas as pl
from jax.experimental.pallas import tpu as pltpu
from jax.sharding import PartitionSpec as P

MESH = pl.DeviceIdType.MESH
F32 = jnp.float32
BF16 = jnp.bfloat16
ROOT_PI = math.sqrt(math.pi)
OWN = 64
WIDE = 128
CENTRE = 16.0
NT = (((1,), (1,)), ((), ()))


def split(x):
    hi = x.astype(BF16).astype(F32)
    return jnp.concatenate([hi, x - hi], axis=0).astype(BF16)


def fold(x):
    half = x.shape[0] // 2
    return x[:half] + x[half:]


def pair_up(first, second):
    low = lax.broadcasted_iota(jnp.int32, first.shape, first.ndim - 1) < OWN
    axis = first.ndim - 1
    return (
        jnp.where(low, first, pltpu.roll(second, OWN, axis)),
        jnp.where(low, pltpu.roll(first, OWN, axis), second),
    )


def ring(n, step):
    return min(step % n, -step % n)


def row_chunks(xs, zs):
    chosen = []
    for dx in range(xs):
        for dz in range(zs):
            back = (-dx % xs, -dz % zs)
            if (dx, dz) <= back:
                weight = 0.5 if (dx, dz) == back else 1.0
                chosen.append((dx, dz, ring(xs, dx) + ring(zs, dz), weight))
    return sorted(chosen, key=lambda c: (c[2], c[0], c[1]))


def kernel(
    xs, zs, cols,
    hard_any, width_any, pos_any, species_any, charge_any, cot_any, warm_any,
    adj_out, grad_out,
    hard_ref, width_ref, pos_ref, species_ref, charge_ref, cot_ref, warm_ref,
    own_geo, own_vec, own_tmp,
    col_g, row_g, col_v, row_v, col_w, row_w, col_p, row_p, col_q, row_q,
    col_ta, row_ta, col_tb, row_tb, col_tc, row_tc, col_s, row_s,
    scal, geo_i, geo_j, vec_i, vec_j, out_i, out_j, grad_i, grad_j,
    bcast, k_hi, k_lo, h_hi, h_lo,
    in_sem, send_sem, recv_sem, chunk_sem,
):
    rows = xs * zs
    ys = cols // 2
    offsets = row_chunks(xs, zs)
    chunks = len(offsets)
    pairs = chunks // 2
    tiles = cols // 2
    near = (pairs + 1) // 2
    row = lax.axis_index("row")
    col = lax.axis_index("col")
    row_x, row_z = row // zs, lax.rem(row, zs)
    col_y, col_core = col // 2, lax.rem(col, 2)

    def at_row(dx, dz):
        return {"row": lax.rem(row_x + dx % xs, xs) * zs + lax.rem(row_z + dz % zs, zs)}

    def at_chunk(k, sign):
        return at_row(sign * offsets[k][0], sign * offsets[k][1])

    def at_col(m, sign):
        core = col_core if m % 2 == 0 else 1 - col_core
        return {"col": 2 * lax.rem(col_y + (sign * (m // 2)) % ys, ys) + core}

    col_far = sorted(range(1, cols), key=lambda m: (-ring(ys, m // 2), m))
    row_far = sorted(range(1, chunks), key=lambda k: -offsets[k][2])
    hops = [(ring(ys, m // 2), "col", m) for m in col_far] + [(offsets[k][2], "row", k) for k in row_far]
    all_far = sorted(hops, key=lambda h: -h[0])

    fetches = [
        pltpu.make_async_copy(source, target, in_sem.at[n])
        for n, (source, target) in enumerate(
            [
                (hard_any, hard_ref), (width_any, width_ref), (pos_any, pos_ref), (species_any, species_ref),
                (charge_any, charge_ref), (cot_any, cot_ref), (warm_any, warm_ref),
            ]
        )
    ]
    for fetch in fetches:
        fetch.start()

    barrier = pltpu.get_barrier_semaphore()
    for _, kind, n in all_far:
        partner = at_col(n, 1) if kind == "col" else at_chunk(n, 1)
        pl.semaphore_signal(barrier, inc=1, device_id=partner, device_id_type=MESH)

    for fetch in fetches:
        fetch.wait()

    lane = lax.broadcasted_iota(jnp.int32, (8, WIDE), 1)
    sub = lax.broadcasted_iota(jnp.int32, (8, WIDE), 0)
    low = lane < OWN
    species = species_ref[...]
    hard = jnp.zeros((1, OWN), F32)
    wide = jnp.zeros((1, OWN), F32)
    for s in range(4):
        hard = hard + jnp.where(species == s, hard_ref[s], 0.0)
        wide = wide + jnp.where(species == s, width_ref[s], 0.0)
    own_geo[...] = jnp.zeros((8, WIDE), F32)
    own_geo[0:3, 0:OWN] = pos_ref[...]
    own_geo[3:4, 0:OWN] = 2.0 * wide * wide
    own_geo[4:5, 0:OWN] = charge_ref[...]
    own_geo[5:6, 0:OWN] = hard + 1.0 / (wide * ROOT_PI)
    own_vec[...] = jnp.zeros((3, 8, WIDE), F32)
    own_vec[0, :, 0:OWN] = warm_ref[...]
    own_tmp[...] = jnp.zeros((8, WIDE), F32)
    own_tmp[:, 0:OWN] = cot_ref[...]
    own = own_geo[...] + pltpu.roll(own_vec[0], OWN, 1)
    col_g[0] = own
    row_g[0] = own

    pl.semaphore_wait(barrier, cols + chunks - 2)

    def copy_col(phase, m, source, target, sign):
        pltpu.make_async_remote_copy(
            src_ref=source, dst_ref=target.at[m],
            send_sem=send_sem.at[2 * phase], recv_sem=recv_sem.at[2 * phase],
            device_id=at_col(m, sign), device_id_type=MESH,
        ).start()

    def copy_row(phase, k, source, target, sign, arrived):
        pltpu.make_async_remote_copy(
            src_ref=source, dst_ref=target.at[k],
            send_sem=send_sem.at[2 * phase + 1], recv_sem=arrived,
            device_id=at_chunk(k, sign), device_id_type=MESH,
        ).start()

    def wait_all(buffer, count, sem):
        part = buffer.at[pl.ds(1, count - 1)]
        pltpu.make_async_copy(part, part, sem).wait()

    def wait_col(phase, target):
        wait_all(target, cols, recv_sem.at[2 * phase])

    def wait_row(phase, target):
        wait_all(target, chunks, recv_sem.at[2 * phase + 1])

    def wait_sent(phase, col_like, row_like, row_count):
        wait_all(col_like, cols, send_sem.at[2 * phase])
        wait_all(row_like, row_count, send_sem.at[2 * phase + 1])

    def gather(phase, turn, col_to, row_to):
        for _, kind, n in all_far:
            if kind == "col":
                copy_col(phase, n, col_to.at[0], col_to, -1)
            else:
                copy_row(phase, n, row_to.at[0], row_to, -1, chunk_sem.at[turn, n])

    def wait_chunk(turn, row_to, k):
        if k > 0:
            pltpu.make_async_copy(row_to.at[k], row_to.at[k], chunk_sem.at[turn, k]).wait()

    def scatter_row(phase, k, source, target):
        copy_row(phase, k, source, target, 1, recv_sem.at[2 * phase + 1])

    def scatter_cols(phase, source, target):
        for m in col_far:
            copy_col(phase, m, source(m), target, 1)

    def weight_of(v):
        return jnp.where(low, offsets[2 * v][3], offsets[2 * v + 1][3]).astype(F32)

    def gathered_sum(source_i, source_j, col_from, row_from):
        even = source_i[0] + source_j[0]
        odd = jnp.zeros_like(even)
        for m in range(1, cols):
            if m % 2:
                odd = odd + col_from[m]
            else:
                even = even + col_from[m]
        for k in range(1, chunks):
            if k % 2:
                odd = odd + row_from[k]
            else:
                even = even + row_from[k]
        return even + pltpu.roll(odd, OWN, 1)

    gather(0, 0, col_g, row_g)
    wait_col(0, col_g)
    for u in range(tiles):
        geo, vec = pair_up(col_g[2 * u], col_g[2 * u + 1])
        geo_i[u] = geo
        vec_i[0, u] = vec

    def all_columns(values):
        return split(jnp.concatenate(values, axis=1))

    def square_of(rows_at, u):
        dx = bcast[0, rows_at, :] - geo_i[u, 0:1, :]
        dy = bcast[1, rows_at, :] - geo_i[u, 1:2, :]
        dz = bcast[2, rows_at, :] - geo_i[u, 2:3, :]
        return dx * dx + dy * dy + dz * dz

    def same_atoms():
        r = lax.broadcasted_iota(jnp.int32, (WIDE, WIDE), 0)
        l = lax.broadcasted_iota(jnp.int32, (WIDE, WIDE), 1)
        return (r == l) & (r < OWN)

    def put(hi_ref, lo_ref, v, u, values):
        lanes = pl.ds(u * WIDE if isinstance(u, int) else pl.multiple_of(u * WIDE, WIDE), WIDE)
        hi = values.astype(BF16)
        lo = (values - hi.astype(F32)).astype(BF16)
        hi_ref[v * WIDE:(v + 1) * WIDE, lanes] = hi
        lo_ref[v * WIDE:(v + 1) * WIDE, lanes] = lo
        return hi, lo

    def coulomb_tile(v, u, same):
        rows_at = pl.ds(v * WIDE, WIDE)
        square = square_of(rows_at, u)
        inverse = lax.rsqrt(bcast[3, rows_at, :] + geo_i[u, 3:4, :])
        if same is not None:
            square = jnp.where(same, 1.0, square)
        recip = lax.rsqrt(square)
        values = lax.erf(inverse * (square * recip)) * recip
        if same is not None:
            values = jnp.where(same, 0.0, values)
        return put(k_hi, k_lo, v, u, values)

    def slope_tile(v, u, same):
        rows_at = pl.ds(v * WIDE, WIDE)
        block = slice(v * WIDE, (v + 1) * WIDE)
        lanes = pl.ds(u * WIDE if isinstance(u, int) else pl.multiple_of(u * WIDE, WIDE), WIDE)
        square = square_of(rows_at, u)
        inverse = lax.rsqrt(bcast[3, rows_at, :] + geo_i[u, 3:4, :])
        if same is not None:
            square = jnp.where(same, 1.0, square)
        recip = lax.rsqrt(square)
        values = k_hi[block, lanes].astype(F32) + k_lo[block, lanes].astype(F32)
        bell = (2.0 / ROOT_PI) * inverse * jnp.exp(-(inverse * inverse) * square)
        values = (bell - values) * (recip * recip)
        if same is not None:
            values = jnp.where(same, 0.0, values)
        put(h_hi, h_lo, v, u, values)

    columns = all_columns([vec_i[0, u] for u in range(tiles)])
    order = list(range(pairs // 3)) + list(range(pairs - 1, pairs // 3 - 1, -1))
    image = jnp.zeros((8, tiles * WIDE), F32)
    for v in order:
        wait_chunk(0, row_g, 2 * v)
        wait_chunk(0, row_g, 2 * v + 1)
        geo, vec = pair_up(row_g[2 * v], row_g[2 * v + 1])
        geo_j[v] = geo
        vec_j[0, v] = vec
        tall = jnp.transpose(geo)
        for f in range(4):
            bcast[f, v * WIDE:(v + 1) * WIDE, :] = jnp.broadcast_to(tall[:, f:f + 1], (WIDE, WIDE))
        first = 0
        if v == 0:
            coulomb_tile(0, 0, same_atoms())
            first = 1

        @pl.loop(first, tiles)
        def _(u):
            coulomb_tile(v, u, None)

        block = slice(v * WIDE, (v + 1) * WIDE)
        over_rows = split(vec * weight_of(v))
        out = jnp.dot(over_rows, k_hi[block, :], preferred_element_type=F32)
        image = image + fold(out + jnp.dot(over_rows, k_lo[block, :], preferred_element_type=F32))
        back = lax.dot_general(columns, k_hi[block, :], NT, preferred_element_type=F32)
        back = back + lax.dot_general(columns, k_lo[block, :], NT, preferred_element_type=F32)
        out_j[0, v] = fold(back) * weight_of(v)
        for k in (2 * v + 1, 2 * v):
            if k > 0:
                scatter_row(1, k, out_j.at[0, v], row_p)

    def put_i(slot, total):
        for u in range(tiles):
            out_i[slot, u] = total[:, u * WIDE:(u + 1) * WIDE]

    put_i(0, image)
    scatter_cols(1, lambda m: out_i.at[0, m // 2], col_p)

    def slopes(part):
        for v in part:
            first = 0
            if v == 0:
                slope_tile(0, 0, same_atoms())
                first = 1

            @pl.loop(first, tiles)
            def _(u):
                slope_tile(v, u, None)

    slopes(range(near))

    diagonal = jnp.where(low, own_geo[5:6, :], 0.0)

    def applied(phase, slot, col_from, row_from):
        wait_col(phase, col_from)
        wait_row(phase, row_from)
        total = gathered_sum(out_i.at[slot], out_j.at[slot], col_from, row_from)
        return jnp.where(low, total, 0.0) + diagonal * own_vec[slot]

    def spread_own(phase, turn, slot, col_to, row_to):
        col_to[0] = own_vec[slot]
        row_to[0] = own_vec[slot]
        gather(phase, turn, col_to, row_to)

    def place_col(phase, slot, col_from):
        wait_col(phase, col_from)
        for u in range(tiles):
            vec_i[slot, u] = pair_up(col_from[2 * u], col_from[2 * u + 1])[0]

    def place_rows(turn, slot, row_from, part):
        for v in part:
            wait_chunk(turn, row_from, 2 * v)
            wait_chunk(turn, row_from, 2 * v + 1)
            vec_j[slot, v] = pair_up(row_from[2 * v], row_from[2 * v + 1])[0]

    def over_rows(slot, part):
        values = split(jnp.concatenate([vec_j[slot, v] * weight_of(v) for v in part], axis=1))
        block = slice(part[0] * WIDE, (part[-1] + 1) * WIDE)
        out = jnp.dot(values, k_hi[block, :], preferred_element_type=F32)
        return fold(out + jnp.dot(values, k_lo[block, :], preferred_element_type=F32))

    def over_columns(values, part):
        block = slice(part[0] * WIDE, (part[-1] + 1) * WIDE)
        out = lax.dot_general(values, k_hi[block, :], NT, preferred_element_type=F32)
        out = fold(out + lax.dot_general(values, k_lo[block, :], NT, preferred_element_type=F32))
        return [out[:, n * WIDE:(n + 1) * WIDE] * weight_of(v) for n, v in enumerate(part)]

    early = list(range(near))
    late = list(range(near, pairs))

    own_vec[1] = jnp.where(low, own_tmp[...], 0.0) - applied(1, 0, col_p, row_p)
    spread_own(2, 1, 1, col_v, row_v)
    slopes(range(near, pairs))

    place_rows(1, 1, row_v, early)
    image = over_rows(1, early)
    place_col(2, 1, col_v)
    columns = all_columns([vec_i[1, u] for u in range(tiles)])
    for part in (late, early):
        for v, values in zip(part, over_columns(columns, part)):
            out_j[1, v] = values
        for k in range(2 * part[-1] + 1, 2 * part[0] - 1, -1):
            if k > 0:
                scatter_row(3, k, out_j.at[1, k // 2], row_q)
    place_rows(1, 1, row_v, late)
    put_i(1, image + over_rows(1, late))
    scatter_cols(3, lambda m: out_i.at[1, m // 2], col_q)

    def moment_rows(geo, values, weight, with_charge):
        spots = geo - CENTRE
        out = [values] + [values * spots[c:c + 1, :] for c in range(3)]
        if with_charge:
            out.append(geo[4:5, :] * jnp.where(sub < 3, spots, jnp.where(sub == 3, 1.0, 0.0)))
        out = jnp.concatenate(out, axis=0)
        return out if weight is None else out * weight[0:1, :]

    def differences(geo, sums, with_charge):
        spots = geo - CENTRE
        x, y, z = (spots[c:c + 1, :] * sums[0:8] - sums[8 + 8 * c:16 + 8 * c] for c in range(3))
        s = spots * sums[35:36] - sums[32:40] if with_charge else z
        return [jnp.concatenate(half, axis=0) for half in zip(pair_up(x, y), pair_up(z, s))]

    def gradient_rows(slot, with_charge, phase, row_to):
        values = all_columns([moment_rows(geo_i[u], vec_i[slot, u], None, with_charge) for u in range(tiles)])
        out = lax.dot_general(values, h_hi[...], NT, preferred_element_type=F32)
        out = fold(out + lax.dot_general(values, h_lo[...], NT, preferred_element_type=F32))
        for v in range(pairs):
            halves = differences(geo_j[v], out[:, v * WIDE:(v + 1) * WIDE] * weight_of(v)[0:1, :], with_charge)
            for n in range(2):
                grad_j[slot, 2 * v + n] = halves[n]
        for k in row_far:
            scatter_row(phase, k, grad_j.at[slot, k], row_to)

    def gradient_cols(slot, with_charge, phase, col_to):
        values = all_columns(
            [moment_rows(geo_j[v], vec_j[slot, v], weight_of(v), with_charge) for v in range(pairs)]
        )
        out = jnp.dot(values, h_hi[...], preferred_element_type=F32)
        out = fold(out + jnp.dot(values, h_lo[...], preferred_element_type=F32))
        for u in range(tiles):
            halves = differences(geo_i[u], out[:, u * WIDE:(u + 1) * WIDE], with_charge)
            for n in range(2):
                grad_i[slot, 2 * u + n] = halves[n]
        scatter_cols(phase, lambda m: grad_i.at[slot, m], col_to)

    gradient_rows(0, True, 6, row_ta)
    gradient_cols(0, True, 6, col_ta)

    own_vec[2] = applied(3, 1, col_q, row_q)
    spread_own(4, 2, 2, col_w, row_w)
    gradient_rows(1, False, 7, row_tb)
    gradient_cols(1, False, 7, col_tb)

    place_col(4, 2, col_w)
    back = over_columns(all_columns([vec_i[2, u] for u in range(tiles)]), early + late)
    place_rows(2, 2, row_w, early + late)
    form = jnp.zeros((8, WIDE), F32)
    for v in range(pairs):
        form = form + vec_j[2, v] * back[v]
    first = own_vec[1]
    second = own_vec[2]
    form = 2.0 * form + diagonal * second * second

    def at_lane(n, values):
        return jnp.where(lane == n, jnp.sum(values, axis=1, keepdims=True), 0.0)

    scal[0] = (
        at_lane(0, first * first) + at_lane(1, first * second) + at_lane(2, second * second) + at_lane(3, form)
    )
    for m in col_far:
        copy_col(5, m, scal.at[0], col_s, 1)
    gradient_rows(2, False, 8, row_tc)
    wait_col(5, col_s)
    total = scal[0]
    for m in range(1, cols):
        total = total + col_s[m]
    scal[1] = total
    others = [(dx, dz) for dx in range(xs) for dz in range(zs) if (dx, dz) != (0, 0)]
    others = sorted(others, key=lambda o: -(ring(xs, o[0]) + ring(zs, o[1])))
    for n, (dx, dz) in enumerate(others):
        pltpu.make_async_remote_copy(
            src_ref=scal.at[1], dst_ref=row_s.at[1 + n],
            send_sem=send_sem.at[11], recv_sem=recv_sem.at[11],
            device_id=at_row(dx, dz), device_id_type=MESH,
        ).start()
    gradient_cols(2, False, 8, col_tc)

    def gradient_sum(slot, phase, col_from, row_from):
        wait_col(phase, col_from)
        wait_row(phase, row_from)
        total = grad_i[slot, 0] + grad_j[slot, 0]
        for m in range(1, cols):
            total = total + col_from[m]
        for k in range(1, chunks):
            total = total + row_from[k]
        xy, zs_ = total[0:8], total[8:16]
        return xy, pltpu.roll(xy, OWN, 1), zs_, pltpu.roll(zs_, OWN, 1)

    grads = [
        gradient_sum(0, 6, col_ta, row_ta),
        gradient_sum(1, 7, col_tb, row_tb),
        gradient_sum(2, 8, col_tc, row_tc),
    ]
    slope_sums = grads[0][3]

    wait_all(row_s, rows, recv_sem.at[11])
    for k in range(1, rows):
        total = total + row_s[k]
    norm_0, curve_0, square_w, form_w = (total[:, n:n + 1] for n in range(4))
    alpha_0 = norm_0 / curve_0
    norm_1 = norm_0 - 2.0 * alpha_0 * curve_0 + alpha_0 * alpha_0 * square_w
    grow = 1.0 + norm_1 / norm_0
    curve_1 = grow * grow * curve_0 - 2.0 * grow * alpha_0 * square_w + alpha_0 * alpha_0 * form_w
    alpha_1 = norm_1 / curve_1
    with_first = alpha_0 + alpha_1 * grow
    with_second = -alpha_1 * alpha_0
    own_adj = own_vec[0] + with_first * first + with_second * second
    adj_out[...] = own_adj[:, 0:OWN]
    charges = own_geo[4:5, :]
    for c in range(3):
        moment = grads[0][c] + with_first * grads[1][c] + with_second * grads[2][c]
        grad = -(own_adj * slope_sums[c:c + 1, :] + charges * moment)
        grad_out[c] = grad[:, 0:OWN]

    wait_sent(0, col_g, row_g, chunks)
    wait_sent(1, col_p, row_p, chunks)
    wait_sent(2, col_v, row_v, chunks)
    wait_sent(3, col_q, row_q, chunks)
    wait_sent(4, col_w, row_w, chunks)
    wait_sent(5, col_s, row_s, rows)
    wait_sent(6, col_ta, row_ta, chunks)
    wait_sent(7, col_tb, row_tb, chunks)
    wait_sent(8, col_tc, row_tc, chunks)


def solution(mesh):
    rows = mesh.shape["row"]
    cols = mesh.shape["col"]
    zs = 8 if rows % 16 == 0 else 4
    xs = rows // zs
    chunks = len(row_chunks(xs, zs))
    pairs = chunks // 2
    tiles = cols // 2

    def local(positions, species, hardness, gauss_width, charges, cotangent, warm_start):
        def buffer(*shape):
            return pltpu.VMEM(shape, F32)

        def both(height):
            return [buffer(cols, height, WIDE), buffer(chunks, height, WIDE)]

        vmem = pl.BlockSpec(memory_space=pltpu.VMEM)
        adjoint, grad = pl.pallas_call(
            functools.partial(kernel, xs, zs, cols),
            out_shape=(
                jax.ShapeDtypeStruct((8, OWN), F32),
                jax.ShapeDtypeStruct((3, 8, OWN), F32),
            ),
            in_specs=[pl.BlockSpec(memory_space=pl.ANY)] * 7,
            out_specs=(vmem, vmem),
            scratch_shapes=[
                pltpu.SMEM((4,), F32), pltpu.SMEM((4,), F32),
                buffer(3, OWN), pltpu.VMEM((1, OWN), jnp.int32), buffer(1, OWN), buffer(8, OWN), buffer(8, OWN),
                buffer(8, WIDE), buffer(3, 8, WIDE), buffer(8, WIDE),
            ]
            + 5 * both(8)
            + 3 * both(16)
            + [buffer(cols, 8, WIDE), buffer(rows, 8, WIDE)]
            + [
                buffer(2, 8, WIDE),
                buffer(tiles, 8, WIDE), buffer(pairs, 8, WIDE),
                buffer(3, tiles, 8, WIDE), buffer(3, pairs, 8, WIDE),
                buffer(2, tiles, 8, WIDE), buffer(2, pairs, 8, WIDE),
                buffer(3, cols, 16, WIDE), buffer(3, chunks, 16, WIDE),
                buffer(4, pairs * WIDE, WIDE),
            ]
            + [pltpu.VMEM((pairs * WIDE, tiles * WIDE), BF16)] * 4
            + [
                pltpu.SemaphoreType.DMA((7,)),
                pltpu.SemaphoreType.DMA((18,)),
                pltpu.SemaphoreType.DMA((18,)),
                pltpu.SemaphoreType.DMA((3, chunks)),
            ],
            compiler_params=pltpu.CompilerParams(
                collective_id=0, has_side_effects=True, vmem_limit_bytes=60 * 1024 * 1024
            ),
        )(
            hardness, gauss_width, positions, species.reshape(1, OWN), charges.reshape(1, OWN), cotangent, warm_start
        )
        return adjoint, jnp.transpose(grad, (1, 0, 2))

    return jax.shard_map(
        local,
        mesh=mesh,
        in_specs=(
            P(None, ("row", "col")),
            P(("row", "col")),
            P(),
            P(),
            P(("row", "col")),
            P(None, ("row", "col")),
            P(None, ("row", "col")),
        ),
        out_specs=(P(None, ("row", "col")), P(None, None, ("row", "col"))),
        check_vma=False,
    )
```

```python
import functools
import math

import jax
import jax.numpy as jnp
from jax import lax
from jax.experimental import pallas as pl
from jax.experimental.pallas import tpu as pltpu
from jax.sharding import PartitionSpec as P

MESH = pl.DeviceIdType.MESH
F32 = jnp.float32
BF16 = jnp.bfloat16
ROOT_PI = math.sqrt(math.pi)
OWN = 64
WIDE = 128
CENTRE = 16.0
NEAR = 3
NT = (((1,), (1,)), ((), ()))


def split(x):
    hi = x.astype(BF16).astype(F32)
    return jnp.concatenate([hi, x - hi], axis=0).astype(BF16)


def fold(x):
    half = x.shape[0] // 2
    return x[:half] + x[half:]


def pair_up(first, second):
    low = lax.broadcasted_iota(jnp.int32, first.shape, first.ndim - 1) < OWN
    axis = first.ndim - 1
    return (
        jnp.where(low, first, pltpu.roll(second, OWN, axis)),
        jnp.where(low, pltpu.roll(first, OWN, axis), second),
    )


def ring(n, step):
    return min(step % n, -step % n)


def wide_tiles(ys):
    return sorted(range(ys), key=lambda dy: (ring(ys, dy), dy))


def tall_chunks(xs, zs):
    chosen = []
    for dx in range(xs):
        for dz in range(zs):
            back = (-dx % xs, -dz % zs)
            if (dx, dz) <= back:
                weight = 0.5 if (dx, dz) == back else 1.0
                chosen.append((ring(xs, dx) + ring(zs, dz), dx, dz, weight))
    return sorted(chosen)


def kernel(
    xs, zs, cols,
    hard_any, width_any, pos_any, species_any, charge_any, cot_any, warm_any,
    adj_out, grad_out,
    hard_ref, width_ref, pos_ref, species_ref, charge_ref, cot_ref, warm_ref,
    own_geo, own_vec, own_tmp,
    col_g, row_g, col_v, row_v, col_w, row_w, col_p, row_p, col_q, row_q,
    col_ta, row_ta, col_tb, row_tb, col_tc, row_tc, col_s, row_s,
    scal, geo_i, geo_j, vec_i, vec_j, out_i, out_j, grad_i, grad_j,
    bcast, k_hi, k_lo, h_hi, h_lo,
    in_sem, send_sem, recv_sem, tile_sem, pair_sem,
):
    ys = cols // 2
    wide_chips = wide_tiles(ys)
    tall_chips = tall_chunks(xs, zs)
    tiles = len(wide_chips)
    slots = 2 * tiles
    chunks = len(tall_chips)
    pairs = chunks // 2
    row = lax.axis_index("row")
    col = lax.axis_index("col")
    row_x, row_z = row // zs, lax.rem(row, zs)
    col_y, col_core = col // 2, lax.rem(col, 2)

    def device(dx, dy, dz, other):
        return {
            "row": lax.rem(row_x + dx % xs, xs) * zs + lax.rem(row_z + dz % zs, zs),
            "col": 2 * lax.rem(col_y + dy % ys, ys) + (1 - col_core if other else col_core),
        }

    def at_slot(m, sign):
        return device(0, sign * wide_chips[m // 2], 0, m % 2 == 1)

    def at_chunk(k, sign):
        _, dx, dz, _ = tall_chips[k]
        return device(sign * dx, 0, sign * dz, False)

    def slot_hops(m):
        return ring(ys, wide_chips[m // 2])

    def chunk_hops(k):
        return tall_chips[k][0]

    slots_far = list(range(slots - 1, 0, -1))
    chunks_far = list(range(chunks - 1, 0, -1))
    hops = [(slot_hops(m), "slot", m) for m in slots_far] + [(chunk_hops(k), "chunk", k) for k in chunks_far]
    all_far = sorted(hops, key=lambda h: -h[0])

    fetches = [
        pltpu.make_async_copy(source, target, in_sem.at[n])
        for n, (source, target) in enumerate(
            [
                (hard_any, hard_ref), (width_any, width_ref), (pos_any, pos_ref), (species_any, species_ref),
                (charge_any, charge_ref), (cot_any, cot_ref), (warm_any, warm_ref),
            ]
        )
    ]
    for fetch in fetches:
        fetch.start()

    barrier = pltpu.get_barrier_semaphore()
    for _, kind, n in all_far:
        partner = at_slot(n, 1) if kind == "slot" else at_chunk(n, 1)
        pl.semaphore_signal(barrier, inc=1, device_id=partner, device_id_type=MESH)

    for fetch in fetches:
        fetch.wait()

    lane = lax.broadcasted_iota(jnp.int32, (8, WIDE), 1)
    sub = lax.broadcasted_iota(jnp.int32, (8, WIDE), 0)
    low = lane < OWN
    species = species_ref[...]
    hard = jnp.zeros((1, OWN), F32)
    wide = jnp.zeros((1, OWN), F32)
    for s in range(4):
        hard = hard + jnp.where(species == s, hard_ref[s], 0.0)
        wide = wide + jnp.where(species == s, width_ref[s], 0.0)
    own_geo[...] = jnp.zeros((8, WIDE), F32)
    own_geo[0:3, 0:OWN] = pos_ref[...]
    own_geo[3:4, 0:OWN] = 2.0 * wide * wide
    own_geo[4:5, 0:OWN] = charge_ref[...]
    own_geo[5:6, 0:OWN] = hard + 1.0 / (wide * ROOT_PI)
    own_vec[...] = jnp.zeros((3, 8, WIDE), F32)
    own_vec[0, :, 0:OWN] = warm_ref[...]
    own_tmp[...] = jnp.zeros((8, WIDE), F32)
    own_tmp[:, 0:OWN] = cot_ref[...]
    own = own_geo[...] + pltpu.roll(own_vec[0], OWN, 1)
    col_g[0] = own
    row_g[0] = own

    pl.semaphore_wait(barrier, slots + chunks - 2)

    def copy_slot(phase, m, source, target, sign, arrived):
        pltpu.make_async_remote_copy(
            src_ref=source, dst_ref=target.at[m],
            send_sem=send_sem.at[2 * phase], recv_sem=arrived,
            device_id=at_slot(m, sign), device_id_type=MESH,
        ).start()

    def copy_chunk(phase, k, source, target, sign, arrived):
        pltpu.make_async_remote_copy(
            src_ref=source, dst_ref=target.at[k],
            send_sem=send_sem.at[2 * phase + 1], recv_sem=arrived,
            device_id=at_chunk(k, sign), device_id_type=MESH,
        ).start()

    def wait_part(buffer, first, count, sem):
        part = buffer.at[pl.ds(first, count)]
        pltpu.make_async_copy(part, part, sem).wait()

    def wait_slots(phase, target):
        wait_part(target, 1, slots - 1, recv_sem.at[2 * phase])

    def wait_chunks(phase, target):
        wait_part(target, 1, chunks - 1, recv_sem.at[2 * phase + 1])

    def wait_sent(phase, slots_like, chunks_like):
        wait_part(slots_like, 1, slots - 1, send_sem.at[2 * phase])
        wait_part(chunks_like, 1, chunks - 1, send_sem.at[2 * phase + 1])

    def gather(phase, turn, slots_to, chunks_to):
        for _, kind, n in all_far:
            if kind == "slot":
                copy_slot(phase, n, slots_to.at[0], slots_to, -1, tile_sem.at[turn, n // 2])
            else:
                copy_chunk(phase, n, slots_to.at[0], chunks_to, -1, pair_sem.at[turn, n // 2])

    def wait_tile(turn, slots_from, u):
        if u == 0:
            wait_part(slots_from, 1, 1, tile_sem.at[turn, 0])
        else:
            wait_part(slots_from, 2 * u, 2, tile_sem.at[turn, u])

    def wait_pair(turn, chunks_from, v):
        if v == 0:
            wait_part(chunks_from, 1, 1, pair_sem.at[turn, 0])
        else:
            wait_part(chunks_from, 2 * v, 2, pair_sem.at[turn, v])

    def scatter_chunk(phase, k, source, target):
        copy_chunk(phase, k, source, target, 1, recv_sem.at[2 * phase + 1])

    def scatter_slots(phase, source, target):
        for m in slots_far:
            copy_slot(phase, m, source(m), target, 1, recv_sem.at[2 * phase])

    def weight_of(v):
        first, second = tall_chips[2 * v][3], tall_chips[2 * v + 1][3]
        return first if first == second else jnp.where(low[0:1, :], first, second).astype(F32)

    def gathered_sum(source_i, source_j, slots_from, chunks_from):
        even = source_i[0] + source_j[0]
        odd = chunks_from[1]
        for m in range(1, slots):
            if m % 2:
                odd = odd + slots_from[m]
            else:
                even = even + slots_from[m]
        for k in range(2, chunks):
            if k % 2:
                odd = odd + chunks_from[k]
            else:
                even = even + chunks_from[k]
        return even + pltpu.roll(odd, OWN, 1)

    gather(0, 0, col_g, row_g)

    def all_columns(values):
        return split(jnp.concatenate(values, axis=1))

    def square_of(rows_at, u):
        dx = bcast[0, rows_at, :] - geo_i[u, 0:1, :]
        dy = bcast[1, rows_at, :] - geo_i[u, 1:2, :]
        dz = bcast[2, rows_at, :] - geo_i[u, 2:3, :]
        return dx * dx + dy * dy + dz * dz

    def same_atoms():
        r = lax.broadcasted_iota(jnp.int32, (WIDE, WIDE), 0)
        l = lax.broadcasted_iota(jnp.int32, (WIDE, WIDE), 1)
        return (r == l) & (r < OWN)

    def put(hi_ref, lo_ref, v, u, values):
        lanes = slice(u * WIDE, (u + 1) * WIDE)
        hi = values.astype(BF16)
        lo = (values - hi.astype(F32)).astype(BF16)
        hi_ref[v * WIDE:(v + 1) * WIDE, lanes] = hi
        lo_ref[v * WIDE:(v + 1) * WIDE, lanes] = lo

    def coulomb_tile(v, u):
        same = same_atoms() if (v, u) == (0, 0) else None
        rows_at = pl.ds(v * WIDE, WIDE)
        square = square_of(rows_at, u)
        inverse = lax.rsqrt(bcast[3, rows_at, :] + geo_i[u, 3:4, :])
        if same is not None:
            square = jnp.where(same, 1.0, square)
        recip = lax.rsqrt(square)
        values = lax.erf(inverse * (square * recip)) * recip
        if same is not None:
            values = jnp.where(same, 0.0, values)
        put(k_hi, k_lo, v, u, values)

    def slope_tile(v, u):
        same = same_atoms() if (v, u) == (0, 0) else None
        rows_at = pl.ds(v * WIDE, WIDE)
        block = slice(v * WIDE, (v + 1) * WIDE)
        lanes = slice(u * WIDE, (u + 1) * WIDE)
        square = square_of(rows_at, u)
        inverse = lax.rsqrt(bcast[3, rows_at, :] + geo_i[u, 3:4, :])
        if same is not None:
            square = jnp.where(same, 1.0, square)
        recip = lax.rsqrt(square)
        values = k_hi[block, lanes].astype(F32) + k_lo[block, lanes].astype(F32)
        bell = (2.0 / ROOT_PI) * inverse * jnp.exp(-(inverse * inverse) * square)
        values = (bell - values) * (recip * recip)
        if same is not None:
            values = jnp.where(same, 0.0, values)
        put(h_hi, h_lo, v, u, values)

    near_tiles = [u for u in range(tiles) if slot_hops(2 * u) <= NEAR]
    far_tiles = [u for u in range(tiles) if u not in near_tiles]
    near_pairs = [v for v in range(pairs) if chunk_hops(2 * v) <= NEAR]
    far_pairs = [v for v in range(pairs) if v not in near_pairs]

    def take_tiles(part):
        for u in part:
            wait_tile(0, col_g, u)
            geo_i[u], vec_i[0, u] = pair_up(col_g[2 * u], col_g[2 * u + 1])

    def take_pairs(part):
        for v in part:
            wait_pair(0, row_g, v)
            geo_j[v], vec_j[0, v] = pair_up(row_g[2 * v], row_g[2 * v + 1])
            tall = jnp.transpose(geo_j[v])
            for f in range(4):
                bcast[f, v * WIDE:(v + 1) * WIDE, :] = jnp.broadcast_to(tall[:, f:f + 1], (WIDE, WIDE))

    take_tiles(near_tiles)
    take_pairs(near_pairs)
    for v in near_pairs:
        for u in near_tiles:
            coulomb_tile(v, u)
    take_tiles(far_tiles)
    take_pairs(far_pairs)
    columns = all_columns([vec_i[0, u] for u in range(tiles)])
    image = jnp.zeros((8, tiles * WIDE), F32)
    for v in far_pairs + near_pairs[::-1]:
        for u in far_tiles if v in near_pairs else range(tiles):
            coulomb_tile(v, u)
        block = slice(v * WIDE, (v + 1) * WIDE)
        back = lax.dot_general(columns, k_hi[block, :], NT, preferred_element_type=F32)
        back = back + lax.dot_general(columns, k_lo[block, :], NT, preferred_element_type=F32)
        out_j[0, v] = fold(back) * weight_of(v)
        for k in (2 * v + 1, 2 * v):
            if k > 0:
                scatter_chunk(1, k, out_j.at[0, v], row_p)
        over_rows = split(vec_j[0, v] * weight_of(v))
        out = jnp.dot(over_rows, k_hi[block, :], preferred_element_type=F32)
        image = image + fold(out + jnp.dot(over_rows, k_lo[block, :], preferred_element_type=F32))

    def put_i(slot, total):
        for u in range(tiles):
            out_i[slot, u] = total[:, u * WIDE:(u + 1) * WIDE]

    put_i(0, image)
    scatter_slots(1, lambda m: out_i.at[0, m // 2], col_p)

    def slopes(part):
        for v in part:
            for u in range(tiles):
                slope_tile(v, u)

    early = list(range(pairs // 2 + 1))
    late = list(range(pairs // 2 + 1, pairs))
    slopes(early)

    diagonal = jnp.where(low, own_geo[5:6, :], 0.0)

    def applied(phase, slot, col_from, row_from):
        wait_slots(phase, col_from)
        wait_chunks(phase, row_from)
        total = gathered_sum(out_i.at[slot], out_j.at[slot], col_from, row_from)
        return jnp.where(low, total, 0.0) + diagonal * own_vec[slot]

    def spread_own(phase, turn, slot, col_to, row_to):
        col_to[0] = own_vec[slot]
        row_to[0] = own_vec[slot]
        gather(phase, turn, col_to, row_to)

    def place_tiles(turn, slot, slots_from):
        for u in range(tiles):
            wait_tile(turn, slots_from, u)
            vec_i[slot, u] = pair_up(slots_from[2 * u], slots_from[2 * u + 1])[0]

    def place_pairs(turn, slot, chunks_from, part):
        for v in part:
            wait_pair(turn, chunks_from, v)
            vec_j[slot, v] = pair_up(chunks_from[2 * v], chunks_from[2 * v + 1])[0]

    def over_rows(slot, part):
        values = split(jnp.concatenate([vec_j[slot, v] * weight_of(v) for v in part], axis=1))
        block = slice(part[0] * WIDE, (part[-1] + 1) * WIDE)
        out = jnp.dot(values, k_hi[block, :], preferred_element_type=F32)
        return fold(out + jnp.dot(values, k_lo[block, :], preferred_element_type=F32))

    def over_columns(values, part):
        block = slice(part[0] * WIDE, (part[-1] + 1) * WIDE)
        out = lax.dot_general(values, k_hi[block, :], NT, preferred_element_type=F32)
        out = fold(out + lax.dot_general(values, k_lo[block, :], NT, preferred_element_type=F32))
        return [out[:, n * WIDE:(n + 1) * WIDE] * weight_of(v) for n, v in enumerate(part)]

    own_vec[1] = jnp.where(low, own_tmp[...], 0.0) - applied(1, 0, col_p, row_p)
    spread_own(2, 1, 1, col_v, row_v)
    slopes(late)

    place_pairs(1, 1, row_v, early)
    image = over_rows(1, early)
    place_tiles(1, 1, col_v)
    columns = all_columns([vec_i[1, u] for u in range(tiles)])
    for part in (late, early):
        for v, values in zip(part, over_columns(columns, part)):
            out_j[1, v] = values
        for k in range(2 * part[-1] + 1, 2 * part[0] - 1, -1):
            if k > 0:
                scatter_chunk(3, k, out_j.at[1, k // 2], row_q)
    place_pairs(1, 1, row_v, late)
    put_i(1, image + over_rows(1, late))
    scatter_slots(3, lambda m: out_i.at[1, m // 2], col_q)

    def moment_rows(geo, values, weight, with_charge):
        spots = geo - CENTRE
        out = [values] + [values * spots[c:c + 1, :] for c in range(3)]
        if with_charge:
            out.append(geo[4:5, :] * jnp.where(sub < 3, spots, jnp.where(sub == 3, 1.0, 0.0)))
        out = jnp.concatenate(out, axis=0)
        return out * weight

    def differences(geo, sums, with_charge):
        spots = geo - CENTRE
        x, y, z = (spots[c:c + 1, :] * sums[0:8] - sums[8 + 8 * c:16 + 8 * c] for c in range(3))
        s = spots * sums[35:36] - sums[32:40] if with_charge else z
        return [jnp.concatenate(half, axis=0) for half in zip(pair_up(x, y), pair_up(z, s))]

    def gradient_rows(slot, with_charge, phase, row_to):
        values = all_columns([moment_rows(geo_i[u], vec_i[slot, u], 1.0, with_charge) for u in range(tiles)])
        out = lax.dot_general(values, h_hi[...], NT, preferred_element_type=F32)
        out = fold(out + lax.dot_general(values, h_lo[...], NT, preferred_element_type=F32))
        for v in range(pairs):
            halves = differences(geo_j[v], out[:, v * WIDE:(v + 1) * WIDE] * weight_of(v), with_charge)
            for n in range(2):
                grad_j[slot, 2 * v + n] = halves[n]
        for k in chunks_far:
            scatter_chunk(phase, k, grad_j.at[slot, k], row_to)

    def gradient_cols(slot, with_charge, phase, col_to):
        values = all_columns(
            [moment_rows(geo_j[v], vec_j[slot, v], weight_of(v), with_charge) for v in range(pairs)]
        )
        out = jnp.dot(values, h_hi[...], preferred_element_type=F32)
        out = fold(out + jnp.dot(values, h_lo[...], preferred_element_type=F32))
        for u in range(tiles):
            halves = differences(geo_i[u], out[:, u * WIDE:(u + 1) * WIDE], with_charge)
            for n in range(2):
                grad_i[slot, 2 * u + n] = halves[n]
        scatter_slots(phase, lambda m: grad_i.at[slot, m], col_to)

    gradient_rows(0, True, 6, row_ta)
    gradient_cols(0, True, 6, col_ta)

    own_vec[2] = applied(3, 1, col_q, row_q)
    spread_own(4, 2, 2, col_w, row_w)
    gradient_rows(1, False, 7, row_tb)
    gradient_cols(1, False, 7, col_tb)

    place_tiles(2, 2, col_w)
    back = over_columns(all_columns([vec_i[2, u] for u in range(tiles)]), early + late)
    place_pairs(2, 2, row_w, early + late)
    form = jnp.zeros((8, WIDE), F32)
    for v in range(pairs):
        form = form + vec_j[2, v] * back[v]
    first = own_vec[1]
    second = own_vec[2]
    form = 2.0 * form + diagonal * second * second

    def at_lanes(n, values):
        return jnp.where(lane == 8 * n + sub, jnp.sum(values, axis=1, keepdims=True), 0.0)

    scalars = at_lanes(0, first * first) + at_lanes(1, first * second) + at_lanes(2, second * second) + at_lanes(3, form)
    scal[0] = jnp.sum(scalars, axis=0, keepdims=True)
    for m in slots_far:
        copy_slot(5, m, scal.at[0], col_s, 1, recv_sem.at[10])
    gradient_rows(2, False, 8, row_tc)
    gradient_cols(2, False, 8, col_tc)
    wait_slots(5, col_s)
    total = scal[0]
    for m in range(1, slots):
        total = total + col_s[m]
    scal[1] = total
    others = [(dx, dz) for dx in range(xs) for dz in range(zs) if (dx, dz) != (0, 0)]
    others = sorted(others, key=lambda o: -(ring(xs, o[0]) + ring(zs, o[1])))
    for n, (dx, dz) in enumerate(others):
        pltpu.make_async_remote_copy(
            src_ref=scal.at[1], dst_ref=row_s.at[n],
            send_sem=send_sem.at[11], recv_sem=recv_sem.at[11],
            device_id=device(dx, 0, dz, False), device_id_type=MESH,
        ).start()

    def gradient_sum(slot, phase, col_from, row_from):
        wait_slots(phase, col_from)
        wait_chunks(phase, row_from)
        total = grad_i[slot, 0] + grad_j[slot, 0]
        for m in range(1, slots):
            total = total + col_from[m]
        for k in range(1, chunks):
            total = total + row_from[k]
        xy, zs_ = total[0:8], total[8:16]
        return xy, pltpu.roll(xy, OWN, 1), zs_, pltpu.roll(zs_, OWN, 1)

    grads = [
        gradient_sum(0, 6, col_ta, row_ta),
        gradient_sum(1, 7, col_tb, row_tb),
        gradient_sum(2, 8, col_tc, row_tc),
    ]
    slope_sums = grads[0][3]

    wait_sent(0, col_g, row_g)
    wait_sent(1, col_p, row_p)
    wait_sent(2, col_v, row_v)
    wait_sent(3, col_q, row_q)
    wait_sent(4, col_w, row_w)
    wait_sent(6, col_ta, row_ta)
    wait_sent(7, col_tb, row_tb)
    wait_sent(8, col_tc, row_tc)
    wait_part(row_s, 0, len(others), recv_sem.at[11])
    total = scal[1]
    for n in range(len(others)):
        total = total + row_s[n]
    total = jnp.broadcast_to(total, (8, WIDE))
    norm_0, curve_0, square_w, form_w = (
        jnp.sum(jnp.where(lane == 8 * n + sub, total, 0.0), axis=1, keepdims=True) for n in range(4)
    )
    alpha_0 = norm_0 / curve_0
    norm_1 = norm_0 - 2.0 * alpha_0 * curve_0 + alpha_0 * alpha_0 * square_w
    grow = 1.0 + norm_1 / norm_0
    curve_1 = grow * grow * curve_0 - 2.0 * grow * alpha_0 * square_w + alpha_0 * alpha_0 * form_w
    alpha_1 = norm_1 / curve_1
    with_first = alpha_0 + alpha_1 * grow
    with_second = -alpha_1 * alpha_0
    own_adj = own_vec[0] + with_first * first + with_second * second
    adj_out[...] = own_adj[:, 0:OWN]
    charges = own_geo[4:5, :]
    for c in range(3):
        moment = grads[0][c] + with_first * grads[1][c] + with_second * grads[2][c]
        grad = -(own_adj * slope_sums[c:c + 1, :] + charges * moment)
        grad_out[c] = grad[:, 0:OWN]

    wait_part(col_s, 1, slots - 1, send_sem.at[10])
    wait_part(row_s, 0, len(others), send_sem.at[11])


def solution(mesh):
    rows = mesh.shape["row"]
    cols = mesh.shape["col"]
    xs = 4
    zs = rows // xs
    tiles = cols // 2
    slots = cols
    chunks = len(tall_chunks(xs, zs))
    pairs = chunks // 2

    def local(positions, species, hardness, gauss_width, charges, cotangent, warm_start):
        def buffer(*shape):
            return pltpu.VMEM(shape, F32)

        def both(height):
            return [buffer(slots, height, WIDE), buffer(chunks, height, WIDE)]

        vmem = pl.BlockSpec(memory_space=pltpu.VMEM)
        adjoint, grad = pl.pallas_call(
            functools.partial(kernel, xs, zs, cols),
            out_shape=(
                jax.ShapeDtypeStruct((8, OWN), F32),
                jax.ShapeDtypeStruct((3, 8, OWN), F32),
            ),
            in_specs=[pl.BlockSpec(memory_space=pltpu.HBM)] * 7,
            out_specs=(vmem, vmem),
            scratch_shapes=[
                pltpu.SMEM((4,), F32), pltpu.SMEM((4,), F32),
                buffer(3, OWN), pltpu.VMEM((1, OWN), jnp.int32), buffer(1, OWN), buffer(8, OWN), buffer(8, OWN),
                buffer(8, WIDE), buffer(3, 8, WIDE), buffer(8, WIDE),
            ]
            + 5 * both(8)
            + 3 * both(16)
            + [buffer(slots, 1, WIDE), buffer(rows, 1, WIDE)]
            + [
                buffer(2, 1, WIDE),
                buffer(tiles, 8, WIDE), buffer(pairs, 8, WIDE),
                buffer(3, tiles, 8, WIDE), buffer(3, pairs, 8, WIDE),
                buffer(2, tiles, 8, WIDE), buffer(2, pairs, 8, WIDE),
                buffer(3, slots, 16, WIDE), buffer(3, chunks, 16, WIDE),
                buffer(4, pairs * WIDE, WIDE),
            ]
            + [pltpu.VMEM((pairs * WIDE, tiles * WIDE), BF16)] * 4
            + [
                pltpu.SemaphoreType.DMA((7,)),
                pltpu.SemaphoreType.DMA((18,)),
                pltpu.SemaphoreType.DMA((18,)),
                pltpu.SemaphoreType.DMA((3, tiles)),
                pltpu.SemaphoreType.DMA((3, pairs)),
            ],
            compiler_params=pltpu.CompilerParams(
                collective_id=0, has_side_effects=True, vmem_limit_bytes=48 * 1024 * 1024
            ),
        )(
            *(
                pltpu.with_memory_space_constraint(a, pltpu.HBM)
                for a in (
                    hardness, gauss_width, positions, species.reshape(1, OWN), charges.reshape(1, OWN), cotangent, warm_start
                )
            )
        )
        return adjoint, jnp.transpose(grad, (1, 0, 2))

    return jax.shard_map(
        local,
        mesh=mesh,
        in_specs=(
            P(None, ("row", "col")),
            P(("row", "col")),
            P(),
            P(),
            P(("row", "col")),
            P(None, ("row", "col")),
            P(None, ("row", "col")),
        ),
        out_specs=(P(None, ("row", "col")), P(None, None, ("row", "col"))),
        check_vma=False,
    )
```

```python
import functools
import math

import jax
import jax.numpy as jnp
from jax import lax
from jax.experimental import pallas as pl
from jax.experimental.pallas import tpu as pltpu
from jax.sharding import PartitionSpec as P

MESH = pl.DeviceIdType.MESH
F32 = jnp.float32
BF16 = jnp.bfloat16
ROOT_PI = math.sqrt(math.pi)
OWN = 64
WIDE = 128
CENTRE = 16.0
DIRECT = 4
NEAR = 2
NT = (((1,), (1,)), ((), ()))


def split(x):
    hi = x.astype(BF16).astype(F32)
    return jnp.concatenate([hi, x - hi], axis=0).astype(BF16)


def fold(x):
    half = x.shape[0] // 2
    return x[:half] + x[half:]


def pair_up(first, second):
    low = lax.broadcasted_iota(jnp.int32, first.shape, first.ndim - 1) < OWN
    axis = first.ndim - 1
    return (
        jnp.where(low, first, pltpu.roll(second, OWN, axis)),
        jnp.where(low, pltpu.roll(first, OWN, axis), second),
    )


def unpack(x):
    return jnp.concatenate([x, pltpu.roll(x, OWN, 1)], axis=0)


def ring(n, step):
    return min(step % n, -step % n)


def wide_tiles(ys):
    return sorted(range(ys), key=lambda dy: (ring(ys, dy), dy))


def tall_chunks(xs, zs):
    chosen = []
    for dx in range(xs // 2 + 1):
        for dz in range(zs):
            back = (-dx % xs, -dz % zs)
            if (dx, dz) > back:
                continue
            hops = ring(xs, dx) + ring(zs, dz)
            if (dx, dz) == back:
                chosen.append((hops, dx, dz, 0.5))
            elif dx == 1:
                chosen.append((hops, dx, dz, 1.0) if ring(zs, dz) < 2 else (hops, -dx, -dz % zs, 1.0))
            else:
                chosen.append((hops, dx, dz if (dz % 2 == 0) == (dx > 0) else -dz % zs, 1.0))
    return sorted(chosen)


def relay_plan(xs, zs, chips):
    plan = {}
    for k, (hops, dx, dz, _) in enumerate(chips):
        if hops <= DIRECT:
            continue
        ways = []
        for n, (first, hx, hz, _) in enumerate(chips):
            gx, gz = (dx - hx) % xs, (dz - hz) % zs
            second = ring(xs, gx) + ring(zs, gz)
            if 0 < first <= DIRECT and chips[n ^ 1][0] <= DIRECT and first + second == hops:
                ways.append((second, -n, gx, gz))
        _, n, gx, gz = min(ways)
        plan[k] = (gx, gz, -n)
    return plan


def kernel(
    xs, zs, cols,
    hard_any, width_any, pos_any, species_any, charge_any, cot_any, warm_any,
    adj_out, grad_out,
    hard_ref, width_ref, pos_ref, species_ref, charge_ref, cot_ref, warm_ref,
    own_geo, own_vec, own_tmp,
    col_g, row_g, col_v, row_v, col_w, row_w, col_p, row_p, col_q, row_q,
    col_ta, row_ta, col_tb, row_tb, col_tc, row_tc, col_s, row_s,
    scal, geo_i, geo_j, vec_i, vec_j, out_i, out_j, grad_i, grad_j,
    bcast, k_hi, k_lo, h_hi, h_lo,
    in_sem, send_sem, recv_sem, tile_sem, pair_sem,
):
    ys = cols // 2
    wide_chips = wide_tiles(ys)
    tall_chips = tall_chunks(xs, zs)
    tiles = len(wide_chips)
    slots = 2 * tiles
    chunks = len(tall_chips)
    pairs = chunks // 2
    row = lax.axis_index("row")
    col = lax.axis_index("col")
    row_x, row_z = row // zs, lax.rem(row, zs)
    col_y, col_core = col // 2, lax.rem(col, 2)

    def device(dx, dy, dz, other):
        return {
            "row": lax.rem(row_x + dx % xs, xs) * zs + lax.rem(row_z + dz % zs, zs),
            "col": 2 * lax.rem(col_y + dy % ys, ys) + (1 - col_core if other else col_core),
        }

    def at_slot(m, sign):
        return device(0, sign * wide_chips[m // 2], 0, m % 2 == 1)

    def at_chunk(k, sign):
        _, dx, dz, _ = tall_chips[k]
        return device(sign * dx, 0, sign * dz, False)

    def slot_hops(m):
        return ring(ys, wide_chips[m // 2])

    def chunk_hops(k):
        return tall_chips[k][0]

    relays = relay_plan(xs, zs, tall_chips)
    slots_far = list(range(slots - 1, 0, -1))
    chunks_far = list(range(chunks - 1, 0, -1))
    hops = [(slot_hops(m), "slot", m) for m in slots_far] + [(chunk_hops(k), "chunk", k) for k in chunks_far]
    all_far = sorted(hops, key=lambda h: -h[0])

    fetches = [
        pltpu.make_async_copy(source, target, in_sem.at[n])
        for n, (source, target) in enumerate(
            [
                (hard_any, hard_ref), (width_any, width_ref), (pos_any, pos_ref), (species_any, species_ref),
                (charge_any, charge_ref), (cot_any, cot_ref), (warm_any, warm_ref),
            ]
        )
    ]
    for fetch in fetches:
        fetch.start()

    barrier = pltpu.get_barrier_semaphore()
    greeted = {(dx % xs, dz % zs) for k, (_, dx, dz, _) in enumerate(tall_chips) if k > 0 and k not in relays}
    greeted = sorted(greeted | {(gx, gz) for gx, gz, _ in relays.values()})
    partners = [at_slot(m, 1) for m in slots_far] + [device(dx, 0, dz, False) for dx, dz in greeted]
    for partner in partners:
        pl.semaphore_signal(barrier, inc=1, device_id=partner, device_id_type=MESH)

    for fetch in fetches:
        fetch.wait()

    lane = lax.broadcasted_iota(jnp.int32, (8, WIDE), 1)
    sub = lax.broadcasted_iota(jnp.int32, (8, WIDE), 0)
    low = lane < OWN
    species = species_ref[...]
    hard = jnp.zeros((1, OWN), F32)
    wide = jnp.zeros((1, OWN), F32)
    for s in range(4):
        hard = hard + jnp.where(species == s, hard_ref[s], 0.0)
        wide = wide + jnp.where(species == s, width_ref[s], 0.0)
    own_geo[...] = jnp.zeros((8, WIDE), F32)
    own_geo[0:3, 0:OWN] = pos_ref[...]
    own_geo[3:4, 0:OWN] = 2.0 * wide * wide
    own_geo[4:5, 0:OWN] = charge_ref[...]
    own_geo[5:6, 0:OWN] = hard + 1.0 / (wide * ROOT_PI)
    own_vec[...] = jnp.zeros((3, 8, WIDE), F32)
    own_vec[0, :, 0:OWN] = warm_ref[...]
    own_tmp[...] = jnp.zeros((8, WIDE), F32)
    own_tmp[:, 0:OWN] = cot_ref[...]
    own = own_geo[...] + pltpu.roll(own_vec[0], OWN, 1)
    col_g[0] = own
    row_g[0] = own

    pl.semaphore_wait(barrier, len(partners))

    def copy_slot(phase, m, source, target, sign, arrived):
        pltpu.make_async_remote_copy(
            src_ref=source, dst_ref=target.at[m],
            send_sem=send_sem.at[2 * phase], recv_sem=arrived,
            device_id=at_slot(m, sign), device_id_type=MESH,
        ).start()

    def copy_chunk(phase, k, source, target, sign, arrived):
        pltpu.make_async_remote_copy(
            src_ref=source, dst_ref=target.at[k],
            send_sem=send_sem.at[2 * phase + 1], recv_sem=arrived,
            device_id=at_chunk(k, sign), device_id_type=MESH,
        ).start()

    def wait_part(buffer, first, count, sem):
        part = buffer.at[pl.ds(first, count)]
        pltpu.make_async_copy(part, part, sem).wait()

    def wait_slots(phase, target):
        wait_part(target, 1, slots - 1, recv_sem.at[2 * phase])

    def wait_chunks(phase, target):
        wait_part(target, 1, chunks - 1, recv_sem.at[2 * phase + 1])

    def wait_sent(phase, slots_like, chunks_like):
        wait_part(slots_like, 1, slots - 1, send_sem.at[2 * phase])
        wait_part(chunks_like, 1, chunks - 1, send_sem.at[2 * phase + 1])

    def gather(phase, turn, slots_to, chunks_to):
        for _, kind, n in all_far:
            if turn == 0 and kind == "chunk" and n in relays:
                continue
            if kind == "slot":
                copy_slot(phase, n, slots_to.at[0], slots_to, -1, tile_sem.at[turn, n // 2])
            else:
                copy_chunk(phase, n, slots_to.at[0], chunks_to, -1, pair_sem.at[turn, n // 2])

    def wait_tile(turn, slots_from, u):
        if u == 0:
            wait_part(slots_from, 1, 1, tile_sem.at[turn, 0])
        else:
            wait_part(slots_from, 2 * u, 2, tile_sem.at[turn, u])

    def wait_pair(turn, chunks_from, v):
        if v == 0:
            wait_part(chunks_from, 1, 1, pair_sem.at[turn, 0])
        else:
            wait_part(chunks_from, 2 * v, 2, pair_sem.at[turn, v])

    def scatter_chunk(phase, k, source, target):
        copy_chunk(phase, k, source, target, 1, recv_sem.at[2 * phase + 1])

    def scatter_slots(phase, source, target):
        for m in slots_far:
            copy_slot(phase, m, source(m), target, 1, recv_sem.at[2 * phase])

    def weight_of(v):
        first, second = tall_chips[2 * v][3], tall_chips[2 * v + 1][3]
        return first if first == second else jnp.where(low[0:1, :], first, second).astype(F32)

    gather(0, 0, col_g, row_g)

    def all_columns(values):
        return split(jnp.concatenate(values, axis=1))

    def square_of(rows_at, u):
        dx = bcast[0, rows_at, :] - geo_i[u, 0:1, :]
        dy = bcast[1, rows_at, :] - geo_i[u, 1:2, :]
        dz = bcast[2, rows_at, :] - geo_i[u, 2:3, :]
        return dx * dx + dy * dy + dz * dz

    def same_atoms():
        r = lax.broadcasted_iota(jnp.int32, (WIDE, WIDE), 0)
        l = lax.broadcasted_iota(jnp.int32, (WIDE, WIDE), 1)
        return (r == l) & (r < OWN)

    def put(hi_ref, lo_ref, v, u, values):
        lanes = slice(u * WIDE, (u + 1) * WIDE)
        hi = values.astype(BF16)
        lo = (values - hi.astype(F32)).astype(BF16)
        hi_ref[v * WIDE:(v + 1) * WIDE, lanes] = hi
        lo_ref[v * WIDE:(v + 1) * WIDE, lanes] = lo

    def coulomb_tile(v, u):
        same = same_atoms() if (v, u) == (0, 0) else None
        rows_at = pl.ds(v * WIDE, WIDE)
        square = square_of(rows_at, u)
        inverse = lax.rsqrt(bcast[3, rows_at, :] + geo_i[u, 3:4, :])
        if same is not None:
            square = jnp.where(same, 1.0, square)
        recip = lax.rsqrt(square)
        values = lax.erf(inverse * (square * recip)) * recip
        if same is not None:
            values = jnp.where(same, 0.0, values)
        put(k_hi, k_lo, v, u, values)

    def slope_tile(v, u):
        same = same_atoms() if (v, u) == (0, 0) else None
        rows_at = pl.ds(v * WIDE, WIDE)
        block = slice(v * WIDE, (v + 1) * WIDE)
        lanes = slice(u * WIDE, (u + 1) * WIDE)
        square = square_of(rows_at, u)
        inverse = lax.rsqrt(bcast[3, rows_at, :] + geo_i[u, 3:4, :])
        if same is not None:
            square = jnp.where(same, 1.0, square)
        recip = lax.rsqrt(square)
        values = k_hi[block, lanes].astype(F32) + k_lo[block, lanes].astype(F32)
        bell = (2.0 / ROOT_PI) * inverse * jnp.exp(-(inverse * inverse) * square)
        values = (bell - values) * (recip * recip)
        if same is not None:
            values = jnp.where(same, 0.0, values)
        put(h_hi, h_lo, v, u, values)

    def pack(tile):
        return pair_up(tile[0:4], tile[4:8])

    near_tiles = [u for u in range(tiles) if slot_hops(2 * u) <= NEAR]
    far_tiles = [u for u in range(tiles) if u not in near_tiles]
    near_pairs = [v for v in range(pairs) if chunk_hops(2 * v) <= NEAR]
    far_pairs = [v for v in range(pairs) if v not in near_pairs]

    passed_pairs = sorted({n // 2 for _, _, n in relays.values()} - set(near_pairs))

    def take_tiles(part):
        for u in part:
            wait_tile(0, col_g, u)
            geo_i[u], vec_i[0, u] = pair_up(col_g[2 * u], col_g[2 * u + 1])

    def take_pairs(part):
        for v in part:
            if v not in passed_pairs:
                wait_pair(0, row_g, v)
            geo_j[v], vec_j[0, v] = pair_up(row_g[2 * v], row_g[2 * v + 1])
            tall = jnp.transpose(geo_j[v])
            for f in range(4):
                bcast[f, v * WIDE:(v + 1) * WIDE, :] = jnp.broadcast_to(tall[:, f:f + 1], (WIDE, WIDE))

    take_tiles(near_tiles)
    take_pairs(near_pairs)
    for v in near_pairs:
        for u in near_tiles:
            coulomb_tile(v, u)
    for v in passed_pairs:
        wait_pair(0, row_g, v)
    for k, (gx, gz, n) in relays.items():
        pltpu.make_async_remote_copy(
            src_ref=row_g.at[n], dst_ref=row_g.at[k],
            send_sem=send_sem.at[1], recv_sem=pair_sem.at[0, k // 2],
            device_id=device(-gx, 0, -gz, False), device_id_type=MESH,
        ).start()
    take_tiles(far_tiles)
    columns = all_columns([vec_i[0, u] for u in range(tiles)])
    image = jnp.zeros((8, tiles * WIDE), F32)
    for v in far_pairs + near_pairs[::-1]:
        if v in far_pairs:
            take_pairs([v])
        for u in far_tiles if v in near_pairs else range(tiles):
            coulomb_tile(v, u)
        block = slice(v * WIDE, (v + 1) * WIDE)
        back = lax.dot_general(columns, k_hi[block, :], NT, preferred_element_type=F32)
        back = back + lax.dot_general(columns, k_lo[block, :], NT, preferred_element_type=F32)
        out_j[0, 2 * v], out_j[0, 2 * v + 1] = pack(fold(back) * weight_of(v))
        for k in (2 * v + 1, 2 * v):
            if k > 0:
                scatter_chunk(1, k, out_j.at[0, k], row_p)
        over_rows = split(vec_j[0, v] * weight_of(v))
        out = jnp.dot(over_rows, k_hi[block, :], preferred_element_type=F32)
        image = image + fold(out + jnp.dot(over_rows, k_lo[block, :], preferred_element_type=F32))

    def put_i(slot, total):
        for u in range(tiles):
            out_i[slot, 2 * u], out_i[slot, 2 * u + 1] = pack(total[:, u * WIDE:(u + 1) * WIDE])

    put_i(0, image)
    scatter_slots(1, lambda m: out_i.at[0, m], col_p)

    def slopes(part):
        for v in part:
            for u in range(tiles):
                slope_tile(v, u)

    early = list(range(pairs // 2 + 1))
    late = list(range(pairs // 2 + 1, pairs))
    slopes(early)

    diagonal = jnp.where(low, own_geo[5:6, :], 0.0)

    def applied(phase, slot, col_from, row_from):
        wait_slots(phase, col_from)
        total = out_i[slot, 0] + out_j[slot, 0]
        for m in range(1, slots):
            total = total + col_from[m]
        wait_chunks(phase, row_from)
        for k in range(1, chunks):
            total = total + row_from[k]
        return jnp.where(low, unpack(total), 0.0) + diagonal * own_vec[slot]

    def spread_own(phase, turn, slot, col_to, row_to):
        packed = pack(own_vec[slot])[0]
        col_to[0] = packed
        row_to[0] = packed
        gather(phase, turn, col_to, row_to)

    def place_tiles(turn, slot, slots_from):
        for u in range(tiles):
            wait_tile(turn, slots_from, u)
            vec_i[slot, u] = jnp.concatenate(pair_up(slots_from[2 * u], slots_from[2 * u + 1]), axis=0)

    def place_pairs(turn, slot, chunks_from, part):
        for v in part:
            wait_pair(turn, chunks_from, v)
            vec_j[slot, v] = jnp.concatenate(pair_up(chunks_from[2 * v], chunks_from[2 * v + 1]), axis=0)

    def over_rows(slot, part):
        values = split(jnp.concatenate([vec_j[slot, v] * weight_of(v) for v in part], axis=1))
        block = slice(part[0] * WIDE, (part[-1] + 1) * WIDE)
        out = jnp.dot(values, k_hi[block, :], preferred_element_type=F32)
        return fold(out + jnp.dot(values, k_lo[block, :], preferred_element_type=F32))

    def over_columns(values, part):
        block = slice(part[0] * WIDE, (part[-1] + 1) * WIDE)
        out = lax.dot_general(values, k_hi[block, :], NT, preferred_element_type=F32)
        out = fold(out + lax.dot_general(values, k_lo[block, :], NT, preferred_element_type=F32))
        return [out[:, n * WIDE:(n + 1) * WIDE] * weight_of(v) for n, v in enumerate(part)]

    own_vec[1] = jnp.where(low, own_tmp[...], 0.0) - applied(1, 0, col_p, row_p)
    spread_own(2, 1, 1, col_v, row_v)
    slopes(late)

    place_pairs(1, 1, row_v, early)
    image = over_rows(1, early)
    place_tiles(1, 1, col_v)
    columns = all_columns([vec_i[1, u] for u in range(tiles)])
    for part in (late, early):
        for v, values in zip(part, over_columns(columns, part)):
            out_j[1, 2 * v], out_j[1, 2 * v + 1] = pack(values)
        for k in range(2 * part[-1] + 1, 2 * part[0] - 1, -1):
            if k > 0:
                scatter_chunk(3, k, out_j.at[1, k], row_q)
    place_pairs(1, 1, row_v, late)
    put_i(1, image + over_rows(1, late))
    scatter_slots(3, lambda m: out_i.at[1, m], col_q)

    def moment_rows(geo, values, weight, with_charge):
        spots = geo - CENTRE
        out = [values] + [values * spots[c:c + 1, :] for c in range(3)]
        if with_charge:
            out.append(geo[4:5, :] * jnp.where(sub < 3, spots, jnp.where(sub == 3, 1.0, 0.0)))
        out = jnp.concatenate(out, axis=0)
        return out * weight

    def differences(geo, sums, with_charge):
        spots = geo - CENTRE
        x, y, z = (spots[c:c + 1, :] * sums[0:8] - sums[8 + 8 * c:16 + 8 * c] for c in range(3))
        s = spots * sums[35:36] - sums[32:40] if with_charge else z
        return [jnp.concatenate(half, axis=0) for half in zip(pair_up(x, y), pair_up(z, s))]

    def gradient_rows(slot, with_charge, phase, row_to):
        values = all_columns([moment_rows(geo_i[u], vec_i[slot, u], 1.0, with_charge) for u in range(tiles)])
        out = lax.dot_general(values, h_hi[...], NT, preferred_element_type=F32)
        out = fold(out + lax.dot_general(values, h_lo[...], NT, preferred_element_type=F32))
        for v in range(pairs):
            halves = differences(geo_j[v], out[:, v * WIDE:(v + 1) * WIDE] * weight_of(v), with_charge)
            for n in range(2):
                grad_j[slot, 2 * v + n] = halves[n]
        for k in chunks_far:
            scatter_chunk(phase, k, grad_j.at[slot, k], row_to)

    def gradient_cols(slot, with_charge, phase, col_to):
        values = all_columns(
            [moment_rows(geo_j[v], vec_j[slot, v], weight_of(v), with_charge) for v in range(pairs)]
        )
        out = jnp.dot(values, h_hi[...], preferred_element_type=F32)
        out = fold(out + jnp.dot(values, h_lo[...], preferred_element_type=F32))
        for u in range(tiles):
            halves = differences(geo_i[u], out[:, u * WIDE:(u + 1) * WIDE], with_charge)
            for n in range(2):
                grad_i[slot, 2 * u + n] = halves[n]
        scatter_slots(phase, lambda m: grad_i.at[slot, m], col_to)

    gradient_rows(0, True, 6, row_ta)
    gradient_cols(0, True, 6, col_ta)

    own_vec[2] = applied(3, 1, col_q, row_q)
    spread_own(4, 2, 2, col_w, row_w)
    gradient_rows(1, False, 7, row_tb)
    gradient_cols(1, False, 7, col_tb)

    place_tiles(2, 2, col_w)
    back = over_columns(all_columns([vec_i[2, u] for u in range(tiles)]), early + late)
    place_pairs(2, 2, row_w, early + late)
    form = jnp.zeros((8, WIDE), F32)
    for v in range(pairs):
        form = form + vec_j[2, v] * back[v]
    first = own_vec[1]
    second = own_vec[2]
    form = 2.0 * form + diagonal * second * second

    def at_lanes(n, values):
        return jnp.where(lane == 8 * n + sub, jnp.sum(values, axis=1, keepdims=True), 0.0)

    scalars = at_lanes(0, first * first) + at_lanes(1, first * second) + at_lanes(2, second * second) + at_lanes(3, form)
    scal[0] = jnp.sum(scalars, axis=0, keepdims=True)
    for m in slots_far:
        copy_slot(5, m, scal.at[0], col_s, 1, recv_sem.at[10])
    gradient_rows(2, False, 8, row_tc)
    gradient_cols(2, False, 8, col_tc)
    wait_slots(5, col_s)
    total = scal[0]
    for m in range(1, slots):
        total = total + col_s[m]
    scal[1] = total
    others = [(dx, dz) for dx in range(xs) for dz in range(zs) if (dx, dz) != (0, 0)]
    others = sorted(others, key=lambda o: -(ring(xs, o[0]) + ring(zs, o[1])))
    for n, (dx, dz) in enumerate(others):
        pltpu.make_async_remote_copy(
            src_ref=scal.at[1], dst_ref=row_s.at[n],
            send_sem=send_sem.at[11], recv_sem=recv_sem.at[11],
            device_id=device(dx, 0, dz, False), device_id_type=MESH,
        ).start()

    def gradient_sum(slot, phase, col_from, row_from):
        wait_slots(phase, col_from)
        wait_chunks(phase, row_from)
        total = grad_i[slot, 0] + grad_j[slot, 0]
        for m in range(1, slots):
            total = total + col_from[m]
        for k in range(1, chunks):
            total = total + row_from[k]
        xy, zs_ = total[0:8], total[8:16]
        return xy, pltpu.roll(xy, OWN, 1), zs_, pltpu.roll(zs_, OWN, 1)

    grads = [
        gradient_sum(0, 6, col_ta, row_ta),
        gradient_sum(1, 7, col_tb, row_tb),
        gradient_sum(2, 8, col_tc, row_tc),
    ]
    slope_sums = grads[0][3]

    wait_sent(0, col_g, row_g)
    wait_sent(1, col_p, row_p)
    wait_sent(2, col_v, row_v)
    wait_sent(3, col_q, row_q)
    wait_sent(4, col_w, row_w)
    wait_sent(6, col_ta, row_ta)
    wait_sent(7, col_tb, row_tb)
    wait_sent(8, col_tc, row_tc)
    wait_part(row_s, 0, len(others), recv_sem.at[11])
    total = scal[1]
    for n in range(len(others)):
        total = total + row_s[n]
    total = jnp.broadcast_to(total, (8, WIDE))
    norm_0, curve_0, square_w, form_w = (
        jnp.sum(jnp.where(lane == 8 * n + sub, total, 0.0), axis=1, keepdims=True) for n in range(4)
    )
    alpha_0 = norm_0 / curve_0
    norm_1 = norm_0 - 2.0 * alpha_0 * curve_0 + alpha_0 * alpha_0 * square_w
    grow = 1.0 + norm_1 / norm_0
    curve_1 = grow * grow * curve_0 - 2.0 * grow * alpha_0 * square_w + alpha_0 * alpha_0 * form_w
    alpha_1 = norm_1 / curve_1
    with_first = alpha_0 + alpha_1 * grow
    with_second = -alpha_1 * alpha_0
    own_adj = own_vec[0] + with_first * first + with_second * second
    adj_out[...] = own_adj[:, 0:OWN]
    charges = own_geo[4:5, :]
    for c in range(3):
        moment = grads[0][c] + with_first * grads[1][c] + with_second * grads[2][c]
        grad = -(own_adj * slope_sums[c:c + 1, :] + charges * moment)
        grad_out[c] = grad[:, 0:OWN]

    wait_part(col_s, 1, slots - 1, send_sem.at[10])
    wait_part(row_s, 0, len(others), send_sem.at[11])


def solution(mesh):
    rows = mesh.shape["row"]
    cols = mesh.shape["col"]
    xs = 4
    zs = rows // xs
    tiles = cols // 2
    slots = cols
    chunks = len(tall_chunks(xs, zs))
    pairs = chunks // 2

    def local(positions, species, hardness, gauss_width, charges, cotangent, warm_start):
        def buffer(*shape):
            return pltpu.VMEM(shape, F32)

        def both(height):
            return [buffer(slots, height, WIDE), buffer(chunks, height, WIDE)]

        vmem = pl.BlockSpec(memory_space=pltpu.VMEM)
        adjoint, grad = pl.pallas_call(
            functools.partial(kernel, xs, zs, cols),
            out_shape=(
                jax.ShapeDtypeStruct((8, OWN), F32),
                jax.ShapeDtypeStruct((3, 8, OWN), F32),
            ),
            in_specs=[pl.BlockSpec(memory_space=pltpu.HBM)] * 7,
            out_specs=(vmem, vmem),
            scratch_shapes=[
                pltpu.SMEM((4,), F32), pltpu.SMEM((4,), F32),
                buffer(3, OWN), pltpu.VMEM((1, OWN), jnp.int32), buffer(1, OWN), buffer(8, OWN), buffer(8, OWN),
                buffer(8, WIDE), buffer(3, 8, WIDE), buffer(8, WIDE),
            ]
            + both(8)
            + 4 * both(4)
            + 3 * both(16)
            + [buffer(slots, 1, WIDE), buffer(rows, 1, WIDE)]
            + [
                buffer(2, 1, WIDE),
                buffer(tiles, 8, WIDE), buffer(pairs, 8, WIDE),
                buffer(3, tiles, 8, WIDE), buffer(3, pairs, 8, WIDE),
                buffer(2, slots, 4, WIDE), buffer(2, chunks, 4, WIDE),
                buffer(3, slots, 16, WIDE), buffer(3, chunks, 16, WIDE),
                buffer(4, pairs * WIDE, WIDE),
            ]
            + [pltpu.VMEM((pairs * WIDE, tiles * WIDE), BF16)] * 4
            + [
                pltpu.SemaphoreType.DMA((7,)),
                pltpu.SemaphoreType.DMA((18,)),
                pltpu.SemaphoreType.DMA((18,)),
                pltpu.SemaphoreType.DMA((3, tiles)),
                pltpu.SemaphoreType.DMA((3, pairs)),
            ],
            compiler_params=pltpu.CompilerParams(
                collective_id=0, has_side_effects=True, vmem_limit_bytes=48 * 1024 * 1024
            ),
        )(
            *(
                pltpu.with_memory_space_constraint(a, pltpu.HBM)
                for a in (
                    hardness, gauss_width, positions, species.reshape(1, OWN), charges.reshape(1, OWN), cotangent, warm_start
                )
            )
        )
        return adjoint, jnp.transpose(grad, (1, 0, 2))

    return jax.shard_map(
        local,
        mesh=mesh,
        in_specs=(
            P(None, ("row", "col")),
            P(("row", "col")),
            P(),
            P(),
            P(("row", "col")),
            P(None, ("row", "col")),
            P(None, ("row", "col")),
        ),
        out_specs=(P(None, ("row", "col")), P(None, None, ("row", "col"))),
        check_vma=False,
    )
```

```python
import functools
import math

import jax
import jax.numpy as jnp
from jax import lax
from jax.experimental import pallas as pl
from jax.experimental.pallas import tpu as pltpu
from jax.sharding import PartitionSpec as P

MESH = pl.DeviceIdType.MESH
F32 = jnp.float32
BF16 = jnp.bfloat16
ROOT_PI = math.sqrt(math.pi)
OWN = 64
WIDE = 128
CENTRE = 16.0
DIRECT = 4
NEAR = 2
NT = (((1,), (1,)), ((), ()))


def split(x):
    hi = x.astype(BF16).astype(F32)
    return jnp.concatenate([hi, x - hi], axis=0).astype(BF16)


def fold(x):
    half = x.shape[0] // 2
    return x[:half] + x[half:]


def pair_up(first, second):
    low = lax.broadcasted_iota(jnp.int32, first.shape, first.ndim - 1) < OWN
    axis = first.ndim - 1
    return (
        jnp.where(low, first, pltpu.roll(second, OWN, axis)),
        jnp.where(low, pltpu.roll(first, OWN, axis), second),
    )


def unpack(x):
    return jnp.concatenate([x, pltpu.roll(x, OWN, 1)], axis=0)


def ring(n, step):
    return min(step % n, -step % n)


def wide_tiles(ys):
    return sorted(range(ys), key=lambda dy: (ring(ys, dy), dy))


def tall_chunks(xs, zs):
    chosen = []
    for dx in range(xs // 2 + 1):
        for dz in range(zs):
            back = (-dx % xs, -dz % zs)
            if (dx, dz) > back:
                continue
            hops = ring(xs, dx) + ring(zs, dz)
            if (dx, dz) == back:
                chosen.append((hops, dx, dz, 0.5))
            elif dx == 1:
                chosen.append((hops, dx, dz, 1.0) if ring(zs, dz) < 2 else (hops, -dx, -dz % zs, 1.0))
            else:
                chosen.append((hops, dx, dz if (dz % 2 == 0) == (dx > 0) else -dz % zs, 1.0))
    return sorted(chosen)


def relay_plan(xs, zs, chips):
    plan = {}
    for k, (hops, dx, dz, _) in enumerate(chips):
        if hops <= DIRECT:
            continue
        ways = []
        for n, (first, hx, hz, _) in enumerate(chips):
            gx, gz = (dx - hx) % xs, (dz - hz) % zs
            second = ring(xs, gx) + ring(zs, gz)
            if 0 < first <= DIRECT and chips[n ^ 1][0] <= DIRECT and first + second == hops:
                ways.append((second, -n, gx, gz))
        _, n, gx, gz = min(ways)
        plan[k] = (gx, gz, -n)
    return plan


def kernel(
    xs, zs, cols,
    hard_any, width_any, pos_any, species_any, charge_any, cot_any, warm_any,
    adj_out, grad_out,
    hard_ref, width_ref, pos_ref, species_ref, charge_ref, cot_ref, warm_ref,
    own_geo, own_vec, own_tmp,
    col_g, row_g, col_v, row_v, col_w, row_w, col_p, row_p, col_q, row_q,
    col_ta, row_ta, col_tb, row_tb, col_tc, row_tc, col_s, row_s,
    scal, geo_i, geo_j, vec_i, vec_j, out_i, out_j, grad_i, grad_j,
    bcast, k_hi, k_lo, h_hi, h_lo,
    in_sem, send_sem, recv_sem, tile_sem, pair_sem,
):
    ys = cols // 2
    wide_chips = wide_tiles(ys)
    tall_chips = tall_chunks(xs, zs)
    tiles = len(wide_chips)
    slots = 2 * tiles
    chunks = len(tall_chips)
    pairs = chunks // 2
    row = lax.axis_index("row")
    col = lax.axis_index("col")
    row_x, row_z = row // zs, lax.rem(row, zs)
    col_y, col_core = col // 2, lax.rem(col, 2)

    def device(dx, dy, dz, other):
        return {
            "row": lax.rem(row_x + dx % xs, xs) * zs + lax.rem(row_z + dz % zs, zs),
            "col": 2 * lax.rem(col_y + dy % ys, ys) + (1 - col_core if other else col_core),
        }

    def at_slot(m, sign):
        return device(0, sign * wide_chips[m // 2], 0, m % 2 == 1)

    def at_chunk(k, sign):
        _, dx, dz, _ = tall_chips[k]
        return device(sign * dx, 0, sign * dz, False)

    def slot_hops(m):
        return ring(ys, wide_chips[m // 2])

    def chunk_hops(k):
        return tall_chips[k][0]

    relays = relay_plan(xs, zs, tall_chips)
    slots_far = list(range(slots - 1, 0, -1))
    chunks_far = list(range(chunks - 1, 0, -1))
    hops = [(slot_hops(m), "slot", m) for m in slots_far] + [(chunk_hops(k), "chunk", k) for k in chunks_far]
    all_far = sorted(hops, key=lambda h: -h[0])

    fetches = [
        pltpu.make_async_copy(source, target, in_sem.at[n])
        for n, (source, target) in enumerate(
            [
                (hard_any, hard_ref), (width_any, width_ref), (pos_any, pos_ref), (species_any, species_ref),
                (charge_any, charge_ref), (cot_any, cot_ref), (warm_any, warm_ref),
            ]
        )
    ]
    for fetch in fetches:
        fetch.start()

    barrier = pltpu.get_barrier_semaphore()
    greeted = {(dx % xs, dz % zs) for k, (_, dx, dz, _) in enumerate(tall_chips) if k > 0 and k not in relays}
    greeted = sorted(greeted | {(gx, gz) for gx, gz, _ in relays.values()})
    partners = [at_slot(m, 1) for m in slots_far] + [device(dx, 0, dz, False) for dx, dz in greeted]
    for partner in partners:
        pl.semaphore_signal(barrier, inc=1, device_id=partner, device_id_type=MESH)

    for fetch in fetches:
        fetch.wait()

    lane = lax.broadcasted_iota(jnp.int32, (8, WIDE), 1)
    sub = lax.broadcasted_iota(jnp.int32, (8, WIDE), 0)
    low = lane < OWN
    species = species_ref[...]
    hard = jnp.zeros((1, OWN), F32)
    wide = jnp.zeros((1, OWN), F32)
    for s in range(4):
        hard = hard + jnp.where(species == s, hard_ref[s], 0.0)
        wide = wide + jnp.where(species == s, width_ref[s], 0.0)
    own_geo[...] = jnp.zeros((8, WIDE), F32)
    own_geo[0:3, 0:OWN] = pos_ref[...]
    own_geo[3:4, 0:OWN] = 2.0 * wide * wide
    own_geo[4:5, 0:OWN] = charge_ref[...]
    own_geo[5:6, 0:OWN] = hard + 1.0 / (wide * ROOT_PI)
    own_vec[...] = jnp.zeros((3, 8, WIDE), F32)
    own_vec[0, :, 0:OWN] = warm_ref[...]
    own_tmp[...] = jnp.zeros((8, WIDE), F32)
    own_tmp[:, 0:OWN] = cot_ref[...]
    own = own_geo[...] + pltpu.roll(own_vec[0], OWN, 1)
    col_g[0] = own
    row_g[0] = own

    pl.semaphore_wait(barrier, len(partners))

    def copy_slot(phase, m, source, target, sign, arrived):
        pltpu.make_async_remote_copy(
            src_ref=source, dst_ref=target.at[m],
            send_sem=send_sem.at[2 * phase], recv_sem=arrived,
            device_id=at_slot(m, sign), device_id_type=MESH,
        ).start()

    def copy_chunk(phase, k, source, target, sign, arrived):
        pltpu.make_async_remote_copy(
            src_ref=source, dst_ref=target.at[k],
            send_sem=send_sem.at[2 * phase + 1], recv_sem=arrived,
            device_id=at_chunk(k, sign), device_id_type=MESH,
        ).start()

    def wait_part(buffer, first, count, sem):
        part = buffer.at[pl.ds(first, count)]
        pltpu.make_async_copy(part, part, sem).wait()

    def wait_slots(phase, target):
        wait_part(target, 1, slots - 1, recv_sem.at[2 * phase])

    def wait_chunks(phase, target):
        wait_part(target, 1, chunks - 1, recv_sem.at[2 * phase + 1])

    def wait_sent(phase, slots_like, chunks_like):
        wait_part(slots_like, 1, slots - 1, send_sem.at[2 * phase])
        wait_part(chunks_like, 1, chunks - 1, send_sem.at[2 * phase + 1])

    def gather(phase, turn, slots_to, chunks_to):
        for _, kind, n in all_far:
            if turn == 0 and kind == "chunk" and n in relays:
                continue
            if kind == "slot":
                copy_slot(phase, n, slots_to.at[0], slots_to, -1, tile_sem.at[turn, n // 2])
            else:
                copy_chunk(phase, n, slots_to.at[0], chunks_to, -1, pair_sem.at[turn, n // 2])

    def wait_tile(turn, slots_from, u):
        if u == 0:
            wait_part(slots_from, 1, 1, tile_sem.at[turn, 0])
        else:
            wait_part(slots_from, 2 * u, 2, tile_sem.at[turn, u])

    def wait_pair(turn, chunks_from, v):
        if v == 0:
            wait_part(chunks_from, 1, 1, pair_sem.at[turn, 0])
        else:
            wait_part(chunks_from, 2 * v, 2, pair_sem.at[turn, v])

    def scatter_chunk(phase, k, source, target):
        copy_chunk(phase, k, source, target, 1, recv_sem.at[2 * phase + 1])

    def scatter_slots(phase, source, target):
        for m in slots_far:
            copy_slot(phase, m, source(m), target, 1, recv_sem.at[2 * phase])

    def weight_of(v):
        first, second = tall_chips[2 * v][3], tall_chips[2 * v + 1][3]
        return first if first == second else jnp.where(low[0:1, :], first, second).astype(F32)

    gather(0, 0, col_g, row_g)

    def all_columns(values):
        return split(jnp.concatenate(values, axis=1))

    def square_of(rows_at, u):
        dx = bcast[0, rows_at, :] - geo_i[u, 0:1, :]
        dy = bcast[1, rows_at, :] - geo_i[u, 1:2, :]
        dz = bcast[2, rows_at, :] - geo_i[u, 2:3, :]
        return dx * dx + dy * dy + dz * dz

    def same_atoms():
        r = lax.broadcasted_iota(jnp.int32, (WIDE, WIDE), 0)
        l = lax.broadcasted_iota(jnp.int32, (WIDE, WIDE), 1)
        return (r == l) & (r < OWN)

    def put(hi_ref, lo_ref, v, u, values):
        lanes = slice(u * WIDE, (u + 1) * WIDE)
        hi = values.astype(BF16)
        lo = (values - hi.astype(F32)).astype(BF16)
        hi_ref[v * WIDE:(v + 1) * WIDE, lanes] = hi
        lo_ref[v * WIDE:(v + 1) * WIDE, lanes] = lo

    def coulomb_tile(v, u):
        same = same_atoms() if (v, u) == (0, 0) else None
        rows_at = pl.ds(v * WIDE, WIDE)
        square = square_of(rows_at, u)
        inverse = lax.rsqrt(bcast[3, rows_at, :] + geo_i[u, 3:4, :])
        if same is not None:
            square = jnp.where(same, 1.0, square)
        recip = lax.rsqrt(square)
        values = lax.erf(inverse * (square * recip)) * recip
        if same is not None:
            values = jnp.where(same, 0.0, values)
        put(k_hi, k_lo, v, u, values)

    def slope_tile(v, u):
        same = same_atoms() if (v, u) == (0, 0) else None
        rows_at = pl.ds(v * WIDE, WIDE)
        block = slice(v * WIDE, (v + 1) * WIDE)
        lanes = slice(u * WIDE, (u + 1) * WIDE)
        square = square_of(rows_at, u)
        inverse = lax.rsqrt(bcast[3, rows_at, :] + geo_i[u, 3:4, :])
        if same is not None:
            square = jnp.where(same, 1.0, square)
        recip = lax.rsqrt(square)
        values = k_hi[block, lanes].astype(F32) + k_lo[block, lanes].astype(F32)
        bell = (2.0 / ROOT_PI) * inverse * jnp.exp(-(inverse * inverse) * square)
        values = (bell - values) * (recip * recip)
        if same is not None:
            values = jnp.where(same, 0.0, values)
        put(h_hi, h_lo, v, u, values)

    def pack(tile):
        return pair_up(tile[0:4], tile[4:8])

    near_tiles = [u for u in range(tiles) if slot_hops(2 * u) <= NEAR]
    far_tiles = [u for u in range(tiles) if u not in near_tiles]
    near_pairs = [v for v in range(pairs) if chunk_hops(2 * v) <= NEAR]
    far_pairs = [v for v in range(pairs) if v not in near_pairs]

    passed_pairs = sorted({n // 2 for _, _, n in relays.values()} - set(near_pairs))

    def take_tiles(part):
        for u in part:
            wait_tile(0, col_g, u)
            geo_i[u], vec_i[0, u] = pair_up(col_g[2 * u], col_g[2 * u + 1])

    def take_pairs(part):
        for v in part:
            if v not in passed_pairs:
                wait_pair(0, row_g, v)
            geo_j[v], vec_j[0, v] = pair_up(row_g[2 * v], row_g[2 * v + 1])
            tall = jnp.transpose(geo_j[v])
            for f in range(4):
                bcast[f, v * WIDE:(v + 1) * WIDE, :] = jnp.broadcast_to(tall[:, f:f + 1], (WIDE, WIDE))

    take_tiles(near_tiles)
    take_pairs(near_pairs)
    for v in near_pairs:
        for u in near_tiles:
            coulomb_tile(v, u)
    for v in passed_pairs:
        wait_pair(0, row_g, v)
    for k, (gx, gz, n) in relays.items():
        pltpu.make_async_remote_copy(
            src_ref=row_g.at[n], dst_ref=row_g.at[k],
            send_sem=send_sem.at[1], recv_sem=pair_sem.at[0, k // 2],
            device_id=device(-gx, 0, -gz, False), device_id_type=MESH,
        ).start()
    take_tiles(far_tiles)
    columns = all_columns([vec_i[0, u] for u in range(tiles)])
    image = jnp.zeros((8, tiles * WIDE), F32)
    for v in far_pairs + near_pairs[::-1]:
        if v in far_pairs:
            take_pairs([v])
        for u in far_tiles if v in near_pairs else range(tiles):
            coulomb_tile(v, u)
        block = slice(v * WIDE, (v + 1) * WIDE)
        back = lax.dot_general(columns, k_hi[block, :], NT, preferred_element_type=F32)
        back = back + lax.dot_general(columns, k_lo[block, :], NT, preferred_element_type=F32)
        out_j[0, 2 * v], out_j[0, 2 * v + 1] = pack(fold(back) * weight_of(v))
        for k in (2 * v + 1, 2 * v):
            if k > 0:
                scatter_chunk(1, k, out_j.at[0, k], row_p)
        over_rows = split(vec_j[0, v] * weight_of(v))
        out = jnp.dot(over_rows, k_hi[block, :], preferred_element_type=F32)
        image = image + fold(out + jnp.dot(over_rows, k_lo[block, :], preferred_element_type=F32))

    def put_i(slot, total):
        for u in range(tiles):
            out_i[slot, 2 * u], out_i[slot, 2 * u + 1] = pack(total[:, u * WIDE:(u + 1) * WIDE])

    put_i(0, image)
    scatter_slots(1, lambda m: out_i.at[0, m], col_p)

    def slopes(part):
        for v in part:
            for u in range(tiles):
                slope_tile(v, u)

    early = list(range(pairs // 2 + 1))
    late = list(range(pairs // 2 + 1, pairs))
    slopes(early)

    diagonal = jnp.where(low, own_geo[5:6, :], 0.0)

    def applied(phase, slot, col_from, row_from):
        wait_slots(phase, col_from)
        total = out_i[slot, 0] + out_j[slot, 0]
        for m in range(1, slots):
            total = total + col_from[m]
        wait_chunks(phase, row_from)
        for k in range(1, chunks):
            total = total + row_from[k]
        return jnp.where(low, unpack(total), 0.0) + diagonal * own_vec[slot]

    def spread_own(phase, turn, slot, col_to, row_to):
        packed = pack(own_vec[slot])[0]
        col_to[0] = packed
        row_to[0] = packed
        gather(phase, turn, col_to, row_to)

    def place_tiles(turn, slot, slots_from):
        for u in range(tiles):
            wait_tile(turn, slots_from, u)
            vec_i[slot, u] = jnp.concatenate(pair_up(slots_from[2 * u], slots_from[2 * u + 1]), axis=0)

    def place_pairs(turn, slot, chunks_from, part):
        for v in part:
            wait_pair(turn, chunks_from, v)
            vec_j[slot, v] = jnp.concatenate(pair_up(chunks_from[2 * v], chunks_from[2 * v + 1]), axis=0)

    def over_rows(slot, part):
        values = split(jnp.concatenate([vec_j[slot, v] * weight_of(v) for v in part], axis=1))
        block = slice(part[0] * WIDE, (part[-1] + 1) * WIDE)
        out = jnp.dot(values, k_hi[block, :], preferred_element_type=F32)
        return fold(out + jnp.dot(values, k_lo[block, :], preferred_element_type=F32))

    def over_columns(values, part):
        block = slice(part[0] * WIDE, (part[-1] + 1) * WIDE)
        out = lax.dot_general(values, k_hi[block, :], NT, preferred_element_type=F32)
        out = fold(out + lax.dot_general(values, k_lo[block, :], NT, preferred_element_type=F32))
        return [out[:, n * WIDE:(n + 1) * WIDE] * weight_of(v) for n, v in enumerate(part)]

    own_vec[1] = jnp.where(low, own_tmp[...], 0.0) - applied(1, 0, col_p, row_p)
    spread_own(2, 1, 1, col_v, row_v)
    slopes(late)

    place_pairs(1, 1, row_v, early)
    image = over_rows(1, early)
    place_tiles(1, 1, col_v)
    columns = all_columns([vec_i[1, u] for u in range(tiles)])
    for part in (late, early):
        for v, values in zip(part, over_columns(columns, part)):
            out_j[1, 2 * v], out_j[1, 2 * v + 1] = pack(values)
        for k in range(2 * part[-1] + 1, 2 * part[0] - 1, -1):
            if k > 0:
                scatter_chunk(3, k, out_j.at[1, k], row_q)
    place_pairs(1, 1, row_v, late)
    put_i(1, image + over_rows(1, late))
    scatter_slots(3, lambda m: out_i.at[1, m], col_q)

    def moment_rows(geo, values, weight, with_charge):
        spots = geo - CENTRE
        out = [values] + [values * spots[c:c + 1, :] for c in range(3)]
        if with_charge:
            out.append(geo[4:5, :] * jnp.where(sub < 3, spots, jnp.where(sub == 3, 1.0, 0.0)))
        out = jnp.concatenate(out, axis=0)
        return out * weight

    def differences(geo, sums, with_charge):
        spots = geo - CENTRE
        x, y, z = (spots[c:c + 1, :] * sums[0:8] - sums[8 + 8 * c:16 + 8 * c] for c in range(3))
        out = [x, y, z]
        if with_charge:
            out.append(spots * sums[35:36] - sums[32:40])
        return list(zip(*(pack(tile) for tile in out)))

    def gradient_rows(slot, with_charge, phase, row_to):
        values = all_columns([moment_rows(geo_i[u], vec_i[slot, u], 1.0, with_charge) for u in range(tiles)])
        out = lax.dot_general(values, h_hi[...], NT, preferred_element_type=F32)
        out = fold(out + lax.dot_general(values, h_lo[...], NT, preferred_element_type=F32))
        for v in range(pairs):
            halves = differences(geo_j[v], out[:, v * WIDE:(v + 1) * WIDE] * weight_of(v), with_charge)
            for n in range(2):
                for c, tile in enumerate(halves[n]):
                    grad_j[slot, 2 * v + n, c] = tile
        for k in chunks_far:
            scatter_chunk(phase, k, grad_j.at[slot, k, pl.ds(0, 4 if with_charge else 3)], row_to)

    def gradient_cols(slot, with_charge, phase, col_to):
        values = all_columns(
            [moment_rows(geo_j[v], vec_j[slot, v], weight_of(v), with_charge) for v in range(pairs)]
        )
        out = jnp.dot(values, h_hi[...], preferred_element_type=F32)
        out = fold(out + jnp.dot(values, h_lo[...], preferred_element_type=F32))
        for u in range(tiles):
            halves = differences(geo_i[u], out[:, u * WIDE:(u + 1) * WIDE], with_charge)
            for n in range(2):
                for c, tile in enumerate(halves[n]):
                    grad_i[slot, 2 * u + n, c] = tile
        scatter_slots(phase, lambda m: grad_i.at[slot, m, pl.ds(0, 4 if with_charge else 3)], col_to)

    gradient_rows(0, True, 6, row_ta)
    gradient_cols(0, True, 6, col_ta)

    own_vec[2] = applied(3, 1, col_q, row_q)
    spread_own(4, 2, 2, col_w, row_w)
    gradient_rows(1, False, 7, row_tb)
    gradient_cols(1, False, 7, col_tb)

    place_tiles(2, 2, col_w)
    back = over_columns(all_columns([vec_i[2, u] for u in range(tiles)]), early + late)
    place_pairs(2, 2, row_w, early + late)
    form = jnp.zeros((8, WIDE), F32)
    for v in range(pairs):
        form = form + vec_j[2, v] * back[v]
    first = own_vec[1]
    second = own_vec[2]
    form = 2.0 * form + diagonal * second * second

    def at_lanes(n, values):
        return jnp.where(lane == 8 * n + sub, jnp.sum(values, axis=1, keepdims=True), 0.0)

    scalars = at_lanes(0, first * first) + at_lanes(1, first * second) + at_lanes(2, second * second) + at_lanes(3, form)
    scal[0] = jnp.sum(scalars, axis=0, keepdims=True)
    for m in slots_far:
        copy_slot(5, m, scal.at[0], col_s, 1, recv_sem.at[10])
    gradient_rows(2, False, 8, row_tc)
    gradient_cols(2, False, 8, col_tc)
    wait_slots(5, col_s)
    total = scal[0]
    for m in range(1, slots):
        total = total + col_s[m]
    scal[1] = total
    others = [(dx, dz) for dx in range(xs) for dz in range(zs) if (dx, dz) != (0, 0)]
    others = sorted(others, key=lambda o: -(ring(xs, o[0]) + ring(zs, o[1])))
    for n, (dx, dz) in enumerate(others):
        pltpu.make_async_remote_copy(
            src_ref=scal.at[1], dst_ref=row_s.at[n],
            send_sem=send_sem.at[11], recv_sem=recv_sem.at[11],
            device_id=device(dx, 0, dz, False), device_id_type=MESH,
        ).start()

    def gradient_sum(slot, phase, col_from, row_from):
        wait_slots(phase, col_from)
        wait_chunks(phase, row_from)
        out = []
        for c in range(4 if slot == 0 else 3):
            total = grad_i[slot, 0, c] + grad_j[slot, 0, c]
            for m in range(1, slots):
                total = total + col_from[m, c]
            for k in range(1, chunks):
                total = total + row_from[k, c]
            out.append(unpack(total))
        return out

    grads = [
        gradient_sum(0, 6, col_ta, row_ta),
        gradient_sum(1, 7, col_tb, row_tb),
        gradient_sum(2, 8, col_tc, row_tc),
    ]
    slope_sums = grads[0][3]

    wait_sent(0, col_g, row_g)
    wait_sent(1, col_p, row_p)
    wait_sent(2, col_v, row_v)
    wait_sent(3, col_q, row_q)
    wait_sent(4, col_w, row_w)
    wait_sent(6, col_ta, row_ta)
    wait_sent(7, col_tb, row_tb)
    wait_sent(8, col_tc, row_tc)
    wait_part(row_s, 0, len(others), recv_sem.at[11])
    total = scal[1]
    for n in range(len(others)):
        total = total + row_s[n]
    total = jnp.broadcast_to(total, (8, WIDE))
    norm_0, curve_0, square_w, form_w = (
        jnp.sum(jnp.where(lane == 8 * n + sub, total, 0.0), axis=1, keepdims=True) for n in range(4)
    )
    alpha_0 = norm_0 / curve_0
    norm_1 = norm_0 - 2.0 * alpha_0 * curve_0 + alpha_0 * alpha_0 * square_w
    grow = 1.0 + norm_1 / norm_0
    curve_1 = grow * grow * curve_0 - 2.0 * grow * alpha_0 * square_w + alpha_0 * alpha_0 * form_w
    alpha_1 = norm_1 / curve_1
    with_first = alpha_0 + alpha_1 * grow
    with_second = -alpha_1 * alpha_0
    own_adj = own_vec[0] + with_first * first + with_second * second
    adj_out[...] = own_adj[:, 0:OWN]
    charges = own_geo[4:5, :]
    for c in range(3):
        moment = grads[0][c] + with_first * grads[1][c] + with_second * grads[2][c]
        grad = -(own_adj * slope_sums[c:c + 1, :] + charges * moment)
        grad_out[c] = grad[:, 0:OWN]

    wait_part(col_s, 1, slots - 1, send_sem.at[10])
    wait_part(row_s, 0, len(others), send_sem.at[11])


def solution(mesh):
    rows = mesh.shape["row"]
    cols = mesh.shape["col"]
    xs = 4
    zs = rows // xs
    tiles = cols // 2
    slots = cols
    chunks = len(tall_chunks(xs, zs))
    pairs = chunks // 2

    def local(positions, species, hardness, gauss_width, charges, cotangent, warm_start):
        def buffer(*shape):
            return pltpu.VMEM(shape, F32)

        def both(height):
            return [buffer(slots, *height, WIDE), buffer(chunks, *height, WIDE)]

        vmem = pl.BlockSpec(memory_space=pltpu.VMEM)
        adjoint, grad = pl.pallas_call(
            functools.partial(kernel, xs, zs, cols),
            out_shape=(
                jax.ShapeDtypeStruct((8, OWN), F32),
                jax.ShapeDtypeStruct((3, 8, OWN), F32),
            ),
            in_specs=[pl.BlockSpec(memory_space=pltpu.HBM)] * 7,
            out_specs=(vmem, vmem),
            scratch_shapes=[
                pltpu.SMEM((4,), F32), pltpu.SMEM((4,), F32),
                buffer(3, OWN), pltpu.VMEM((1, OWN), jnp.int32), buffer(1, OWN), buffer(8, OWN), buffer(8, OWN),
                buffer(8, WIDE), buffer(3, 8, WIDE), buffer(8, WIDE),
            ]
            + both((8,))
            + 4 * both((4,))
            + both((4, 4))
            + 2 * both((3, 4))
            + [buffer(slots, 1, WIDE), buffer(rows, 1, WIDE)]
            + [
                buffer(2, 1, WIDE),
                buffer(tiles, 8, WIDE), buffer(pairs, 8, WIDE),
                buffer(3, tiles, 8, WIDE), buffer(3, pairs, 8, WIDE),
                buffer(2, slots, 4, WIDE), buffer(2, chunks, 4, WIDE),
                buffer(3, slots, 4, 4, WIDE), buffer(3, chunks, 4, 4, WIDE),
                buffer(4, pairs * WIDE, WIDE),
            ]
            + [pltpu.VMEM((pairs * WIDE, tiles * WIDE), BF16)] * 4
            + [
                pltpu.SemaphoreType.DMA((7,)),
                pltpu.SemaphoreType.DMA((18,)),
                pltpu.SemaphoreType.DMA((18,)),
                pltpu.SemaphoreType.DMA((3, tiles)),
                pltpu.SemaphoreType.DMA((3, pairs)),
            ],
            compiler_params=pltpu.CompilerParams(
                collective_id=0, has_side_effects=True, vmem_limit_bytes=48 * 1024 * 1024
            ),
        )(
            *(
                pltpu.with_memory_space_constraint(a, pltpu.HBM)
                for a in (
                    hardness, gauss_width, positions, species.reshape(1, OWN), charges.reshape(1, OWN), cotangent, warm_start
                )
            )
        )
        return adjoint, jnp.transpose(grad, (1, 0, 2))

    return jax.shard_map(
        local,
        mesh=mesh,
        in_specs=(
            P(None, ("row", "col")),
            P(("row", "col")),
            P(),
            P(),
            P(("row", "col")),
            P(None, ("row", "col")),
            P(None, ("row", "col")),
        ),
        out_specs=(P(None, ("row", "col")), P(None, None, ("row", "col"))),
        check_vma=False,
    )
```
